512 devices in a mesh: dp: 32 (over z, core), seq: 16 (over y, x).
Axes of the slice: x: 4, y: 4, z: 16, core: 2. Of those that a mesh axis runs over, the one named last changes fastest.
Arguments:
- features: bfloat16 [32, 2048, 512], P('dp', 'seq'), may hold values from -8 to 8
- mask_token: bfloat16 [512], replicated, may hold values from -6 to 6
- w_query: bfloat16 [512, 512], replicated, may hold values from -0.25 to 0.25
- w_key: bfloat16 [512, 512], replicated, may hold values from -0.25 to 0.25
- w_value: bfloat16 [512, 512], replicated, may hold values from -0.25 to 0.25
- block_mask: int32 [32, 16, 16], P('dp'), may hold values from 0 to 1, as said below
- masked_ids: int32 [32, 1024], P('dp'), may hold values from 0 to 2047, as said below
- adjacency: int32 [32, 2048, 128], P('dp', 'seq'), may hold values from 0 to 1, as said below
- boundary_ids: int32 [32, 2, 512], P('dp', None, 'seq'), may hold values from 0 to 127, as said below
- boundary_counts: int32 [32, 2, 16], P('dp', None, 'seq'), may hold values from 1 to 32, as said below
- boundary_targets: int32 [32, 2, 512], P('dp', None, 'seq'), may hold values from 0 to 127
- grad_out: bfloat16 [32, 2048, 512], P('dp', 'seq'), may hold values from -6 to 6
Outputs:
- mixed: bfloat16 [32, 2048, 512], P('dp', 'seq')
- grad_query: float32 [512, 512], P(None, 'seq')
- grad_key: float32 [512, 512], P(None, 'seq')
- grad_value: float32 [512, 512], P(None, 'seq')
The draws below stay inside these ranges and needn't reach their ends.
Inputs may be any that keep to these rules, and one draw needn't show every extreme that they name: `block_mask`: entries are 0 or 1; every diagonal block is 1. `masked_ids`: the ids of one cluster are distinct. `adjacency`: entries are 0 or 1; a row has no link to itself. `boundary_ids`: indices of rows within the sending device's block; the 32 slots of one block and direction are distinct; only the first boundary_counts slots are used by the receiver. `boundary_counts`: some block takes exactly 32 rows in every draw.
All inputs are finite; a program needn't handle non-finite values.
Results may differ from the reference program's by a relative error of at most 0.015.
The reference program's roundings to bfloat16 on the way count: a program that leaves them out, or rounds other values in their place, can miss the bound.
Values may be sent and summed in bfloat16 or wider, within the bound.
No kernel may reach another device: no remote copies, remote signals or barrier semaphores. Data moves between devices by JAX's collectives and lax.ppermute only.
A program may use at most 64 MiB of HBM per device.

```python
import jax
import jax.numpy as jnp
from jax import lax

D = 512
HEADS = 16
BLK = 128
ROWS_DEV = 128
BMAX = 32
S = 2048
NB = 16
MASKED = 1024
CLUSTERS = 32
BROWS = 512
N_SEQ = 16


def draw_features(key, part):
    key = jax.random.fold_in(key, 11)
    shape = (CLUSTERS, S, D)
    return jnp.clip(jax.random.normal(key, shape, jnp.float32), -6.0, 6.0).astype(jnp.bfloat16)


def draw_block_mask(key, part):
    key = jax.random.fold_in(key, 12)
    picks = jax.random.randint(key, (CLUSTERS, NB, NB), 0, 10) == 0
    diagonal = jnp.eye(NB, dtype=jnp.int32)[None, :, :] > 0
    return (picks | diagonal).astype(jnp.int32)


def draw_masked_ids(key, part):
    key = jax.random.fold_in(key, 13)
    keys = jax.random.split(key, CLUSTERS)
    return jax.vmap(lambda item: jax.random.permutation(item, S)[:MASKED])(keys).astype(jnp.int32)


def draw_adjacency(key, part):
    key = jax.random.fold_in(key, 14)
    picks = jax.random.randint(key, (CLUSTERS, S, ROWS_DEV), 0, 8) == 0
    local = jnp.arange(S) % ROWS_DEV
    other = local[:, None] != jnp.arange(ROWS_DEV)[None, :]
    return (picks & other[None, :, :]).astype(jnp.int32)


def draw_boundary_ids(key, part):
    key = jax.random.fold_in(key, 15)
    keys = jax.random.split(key, CLUSTERS * 2 * N_SEQ)
    rows = jax.vmap(lambda item: jax.random.permutation(item, ROWS_DEV)[:BMAX])(keys)
    return rows.reshape(CLUSTERS, 2, BROWS).astype(jnp.int32)


def draw_boundary_counts(key, part):
    key = jax.random.fold_in(key, 16)
    counts = jax.random.randint(key, (CLUSTERS, 2, N_SEQ), 1, BMAX + 1)
    return counts.at[0, 1, 0].set(BMAX).astype(jnp.int32)


def set_ends(values, key, least, high):
    extent = values.shape
    place = [jax.random.randint(jax.random.fold_in(key, axis), (), 0, extent[axis]) for axis in range(len(extent))]
    values = values.at[tuple(place)].set(least)
    longest = extent.index(max(extent))
    place[longest] = (place[longest] + 1) % extent[longest]
    return values.at[tuple(place)].set(high)


def level_of(key, extent, pieces, smallest, largest):
    gain, own = 1.0, jax.random.fold_in(key, 6)
    for position, shards_of in pieces:
        heights = jnp.exp(jax.random.uniform(jax.random.fold_in(own, position), (shards_of,), jnp.float32, smallest / len(pieces), largest / len(pieces)))
        gain = gain * jnp.repeat(heights, extent[position] // shards_of).reshape([-1 if axis == position else 1 for axis in range(len(extent))])
    return gain


def bell_draw(own_key, dims, deviation, bound, cuts=(), kind=jnp.bfloat16):
    result = deviation * jax.random.normal(own_key, dims, jnp.float32)
    if cuts:
        result = result * level_of(own_key, dims, cuts, -0.22, 0.18)
    return jnp.clip(result, -bound, bound).astype(kind)


def setup_inputs(seed: int = 0) -> dict:
    arg_keys = jax.random.split(jax.random.key(seed), 13)
    features = draw_features(jax.random.fold_in(arg_keys[12], 71), 0)
    mask_token = bell_draw(arg_keys[1], (D,), 1.0, 6.0)
    w_query = bell_draw(arg_keys[2], (D, D), D ** -0.5, 0.25)
    w_key = bell_draw(arg_keys[3], (D, D), D ** -0.5, 0.25)
    w_value = bell_draw(arg_keys[4], (D, D), D ** -0.5, 0.25)
    block_mask = draw_block_mask(jax.random.fold_in(arg_keys[12], 71), 0)
    masked_ids = draw_masked_ids(jax.random.fold_in(arg_keys[12], 71), 0)
    adjacency = draw_adjacency(jax.random.fold_in(arg_keys[12], 71), 0)
    boundary_ids = draw_boundary_ids(jax.random.fold_in(arg_keys[12], 71), 0)
    boundary_counts = draw_boundary_counts(jax.random.fold_in(arg_keys[12], 71), 0)
    boundary_targets = set_ends(jax.random.randint(arg_keys[10], (CLUSTERS, 2, BROWS), 0, ROWS_DEV), jax.random.fold_in(arg_keys[10], 1), 0, ROWS_DEV - 1).astype(jnp.int32)
    grad_out = bell_draw(arg_keys[11], (CLUSTERS, S, D), 1.0, 6.0, ((0, 32), (1, 16)))
    return dict(features=features, mask_token=mask_token, w_query=w_query, w_key=w_key, w_value=w_value, block_mask=block_mask, masked_ids=masked_ids, adjacency=adjacency, boundary_ids=boundary_ids, boundary_counts=boundary_counts, boundary_targets=boundary_targets, grad_out=grad_out)


NEG_FILL = -1.0e30


def block_allowed(block_table, start, height, block_size):
    table_rows = lax.dynamic_slice_in_dim(block_table, start // block_size, height // block_size, 0)
    spread = jnp.repeat(jnp.repeat(table_rows, block_size, axis=0), block_size, axis=1)
    return spread > 0


def head_probs(query, keys, block_table, start, height, block_size):
    query_part = lax.dynamic_slice_in_dim(query, start, height, 1)
    scores = lax.dot_general(query_part, keys, (((0,), (0,)), ((), ())), preferred_element_type=jnp.float32)
    scores = scores * (query.shape[0] ** -0.5)
    allowed = block_allowed(block_table, start, height, block_size)
    scores = jnp.where(allowed, scores, NEG_FILL)
    highest = jnp.max(scores, axis=1, keepdims=True)
    expo = jnp.exp(scores - highest)
    return query_part, expo / jnp.sum(expo, axis=1, keepdims=True)


def head_forward(query, keys, values, block_table, block_size):
    total = query.shape[1]
    height = min(512, total)
    count = total // height

    def one_block(index):
        start = index * height
        unused, probs = head_probs(query, keys, block_table, start, height, block_size)
        probs_low = probs.astype(jnp.bfloat16)
        return lax.dot_general(values, probs_low, (((1,), (1,)), ((), ())), preferred_element_type=jnp.float32).astype(jnp.bfloat16)

    blocks = lax.map(one_block, jnp.arange(count).astype(jnp.int32))
    return jnp.transpose(blocks, (1, 0, 2)).reshape(query.shape[0], total)


def head_backward(query, keys, values, grad_head, block_table, block_size):
    total = query.shape[1]
    height = min(512, total)
    count = total // height
    scale = query.shape[0] ** -0.5

    def one_block(carry, index):
        key_acc, value_acc = carry
        start = index * height
        query_part, probs = head_probs(query, keys, block_table, start, height, block_size)
        probs_low = probs.astype(jnp.bfloat16)
        grad_part = lax.dynamic_slice_in_dim(grad_head, start, height, 1)
        grad_probs = lax.dot_general(grad_part, values, (((0,), (0,)), ((), ())), preferred_element_type=jnp.float32)
        inner = jnp.sum(grad_probs * probs, axis=1, keepdims=True)
        grad_scores = (probs * (grad_probs - inner) * scale).astype(jnp.bfloat16)
        grad_query = lax.dot_general(keys, grad_scores, (((1,), (1,)), ((), ())), preferred_element_type=jnp.float32).astype(jnp.bfloat16)
        key_acc = key_acc + lax.dot_general(query_part, grad_scores, (((1,), (0,)), ((), ())), preferred_element_type=jnp.float32)
        value_acc = value_acc + lax.dot_general(grad_part, probs_low, (((1,), (0,)), ((), ())), preferred_element_type=jnp.float32)
        return (key_acc, value_acc), grad_query

    zeros = jnp.zeros(query.shape, jnp.float32)
    (key_acc, value_acc), query_blocks = lax.scan(one_block, (zeros, zeros), jnp.arange(count).astype(jnp.int32))
    grad_query = jnp.transpose(query_blocks, (1, 0, 2)).reshape(query.shape[0], total)
    return grad_query, key_acc.astype(jnp.bfloat16), value_acc.astype(jnp.bfloat16)


def reference(features, mask_token, w_query, w_key, w_value, block_mask, masked_ids, adjacency, boundary_ids, boundary_counts, boundary_targets, grad_out):
    clusters = features.shape[0]
    total = features.shape[1]
    width = features.shape[2]
    rows_dev = total // N_SEQ
    head_size = width // HEADS
    marks = jnp.zeros((clusters, total), jnp.int32).at[jnp.arange(clusters)[:, None], masked_ids].set(1)
    masked = jnp.where(marks[:, :, None] > 0, mask_token[None, None, :], features)
    flat = masked.reshape(clusters * total, width)

    def project(weight):
        return jnp.dot(flat, weight, preferred_element_type=jnp.float32).astype(jnp.bfloat16)

    query_rows = project(w_query)
    key_rows = project(w_key)
    value_rows = project(w_value)

    def to_heads(rows):
        return jnp.transpose(rows.reshape(clusters, total, HEADS, head_size), (0, 2, 3, 1))

    def to_rows(heads):
        return jnp.transpose(heads, (0, 3, 1, 2)).reshape(clusters, total, width)

    def per_cluster(items):
        query_c, key_c, value_c, grad_c, table_c = items
        attend = jax.vmap(lambda a, b, c: head_forward(a, b, c, table_c, BLK))(query_c, key_c, value_c)
        grads = jax.vmap(lambda a, b, c, d: head_backward(a, b, c, d, table_c, BLK))(query_c, key_c, value_c, grad_c)
        return (attend, grads[0], grads[1], grads[2])

    attend, grad_query_h, grad_key_h, grad_value_h = lax.map(per_cluster, (to_heads(query_rows), to_heads(key_rows), to_heads(value_rows), to_heads(grad_out), block_mask))

    values_grid = value_rows.reshape(clusters, N_SEQ, rows_dev, width)
    values_wide = values_grid.astype(jnp.float32)
    links = adjacency.reshape(clusters, N_SEQ, rows_dev, rows_dev).astype(jnp.float32)
    local_sum = values_wide + jnp.einsum('csij,csjd->csid', links, values_wide, precision=lax.Precision.HIGHEST)
    send_ids = boundary_ids.reshape(clusters, 2, N_SEQ, BMAX)
    cluster_index = jnp.arange(clusters).astype(jnp.int32)
    block_index = jnp.arange(N_SEQ).astype(jnp.int32)
    outgoing = values_grid[cluster_index[:, None, None, None], block_index[None, None, :, None], send_ids]
    empty = jnp.zeros_like(outgoing[:1, 0])
    from_lower = jnp.concatenate([empty, outgoing[:-1, 0]], axis=0)
    from_upper = jnp.concatenate([outgoing[1:, 1], empty], axis=0)
    slots = jnp.arange(BMAX).astype(jnp.int32)
    valid_lower = (slots[None, None, :] < boundary_counts[:, 0, :, None]) & (cluster_index[:, None, None] > 0)
    valid_upper = (slots[None, None, :] < boundary_counts[:, 1, :, None]) & (cluster_index[:, None, None] < clusters - 1)
    targets = boundary_targets.reshape(clusters, 2, N_SEQ, BMAX)
    positions = jnp.arange(rows_dev).astype(jnp.int32)
    pick_lower = ((targets[:, 0, :, None, :] == positions[None, None, :, None]) & valid_lower[:, :, None, :]).astype(jnp.float32)
    pick_upper = ((targets[:, 1, :, None, :] == positions[None, None, :, None]) & valid_upper[:, :, None, :]).astype(jnp.float32)
    border = jnp.einsum('csij,csjd->csid', pick_lower, from_lower.astype(jnp.float32), precision=lax.Precision.HIGHEST)
    border = border + jnp.einsum('csij,csjd->csid', pick_upper, from_upper.astype(jnp.float32), precision=lax.Precision.HIGHEST)
    degree = 1.0 + jnp.sum(links, axis=-1) + jnp.sum(pick_lower, axis=-1) + jnp.sum(pick_upper, axis=-1)
    graph = ((local_sum + border) / degree[..., None]).reshape(clusters, total, width)
    mixed = (to_rows(attend).astype(jnp.float32) + graph).astype(jnp.bfloat16)

    scaled = grad_out.astype(jnp.float32).reshape(clusters, N_SEQ, rows_dev, width) / degree[..., None]
    graph_grad = (scaled + jnp.einsum('csji,csjd->csid', links, scaled, precision=lax.Precision.HIGHEST)).astype(jnp.bfloat16)
    graph_grad = graph_grad.reshape(clusters, total, width)
    value_grad = (to_rows(grad_value_h).astype(jnp.float32) + graph_grad.astype(jnp.float32)).astype(jnp.bfloat16)
    grad_query = jnp.dot(flat.T, to_rows(grad_query_h).reshape(clusters * total, width), preferred_element_type=jnp.float32)
    grad_key = jnp.dot(flat.T, to_rows(grad_key_h).reshape(clusters * total, width), preferred_element_type=jnp.float32)
    grad_value = jnp.dot(flat.T, value_grad.reshape(clusters * total, width), preferred_element_type=jnp.float32)
    return (mixed, grad_query, grad_key, grad_value)
```

```python
import jax
import jax.numpy as jnp
from jax import lax
from jax.experimental import pallas as pl
from jax.experimental.pallas import tpu as pltpu
from jax.sharding import PartitionSpec as P

HEADS = 16
NB = 16
BLK = 128
HD = 32
ROWS = 128
WIDTH = 512
UNROLL = 4
SLOTS = NB * NB + UNROLL
SCALE = HD**-0.5
LOG2E = 1.4426950408889634
EXP_SCALE = SCALE * LOG2E
LOWEST = -3e38
BF = jnp.bfloat16
F32 = jnp.float32
CHIPS = 16
CHUNK = 12

SM = pl.BlockSpec(memory_space=pltpu.SMEM)
VM = pl.BlockSpec(memory_space=pltpu.VMEM)


def attach(targets, counts_ref, place_ref, side):
    slots = targets.shape[1]
    rows = lax.broadcasted_iota(jnp.int32, (ROWS, slots), 0)
    slot = lax.broadcasted_iota(jnp.int32, (ROWS, slots), 1)
    inside = (place_ref[0] > 0) if side == 0 else (place_ref[0] < place_ref[2] - 1)
    limit = jnp.where(inside, counts_ref[0, side, 0], 0)
    return jnp.where((targets == rows) & (slot < limit), 1.0, 0.0)


def rows_kernel(
    place_ref, counts_ref, tokens_ref, token_ref, wq_ref, wk_ref, wv_ref, ids_ref, links_ref,
    sends_ref, targets_ref, grad_ref, masked_ref, heads_ref, out_ref, local_ref, degree_ref,
):
    own = place_ref[1] * ROWS + lax.broadcasted_iota(jnp.int32, (ROWS, 128), 0)
    hit = own < 0
    for part in range(ids_ref.shape[1] // 128):
        hit = hit | (own == ids_ref[:, part * 128 : (part + 1) * 128])
    marked = jnp.max(jnp.where(hit, 1.0, 0.0), axis=1, keepdims=True) > 0
    masked = jnp.where(marked, token_ref[...].astype(F32), tokens_ref[0].astype(F32)).astype(BF)
    masked_ref[...] = masked

    links_low = links_ref[0].astype(F32).astype(BF)
    value_wide = jnp.dot(masked, wv_ref[...], preferred_element_type=F32)
    value = value_wide.astype(BF)
    local_ref[...] = value.astype(F32) + jnp.dot(links_low, value, preferred_element_type=F32)
    pick = lax.broadcasted_iota(jnp.int32, (ROWS, 32), 0)
    for side in range(2):
        onehot = jnp.where(sends_ref[0, side : side + 1, :] == pick, 1.0, 0.0).astype(BF)
        out_ref[side] = lax.dot_general(
            onehot, value, (((0,), (0,)), ((), ())), preferred_element_type=F32
        ).astype(BF)

    degree = 1.0 + jnp.sum(links_ref[0].astype(F32), axis=1, keepdims=True)
    for side in range(2):
        links_here = attach(targets_ref[0, side : side + 1, :], counts_ref, place_ref, side)
        degree = degree + jnp.sum(links_here, axis=1, keepdims=True)
    degree_ref[...] = degree

    scaled = (grad_ref[0].astype(F32) / degree).T
    high = scaled.astype(BF)
    rest = scaled - high.astype(F32)
    mid = rest.astype(BF)
    low = (rest - mid.astype(F32)).astype(BF)
    spread = jnp.dot(low, links_low, preferred_element_type=F32)
    spread = spread + jnp.dot(mid, links_low, preferred_element_type=F32)
    spread = spread + jnp.dot(high, links_low, preferred_element_type=F32)
    graph_grad = (scaled + spread).astype(BF)

    key = jnp.dot(masked, wk_ref[...], preferred_element_type=F32).T.astype(BF)
    query = jnp.dot(masked, wq_ref[...], preferred_element_type=F32).T.astype(BF)
    value_t = value_wide.T.astype(BF)
    grad_t = grad_ref[0].astype(F32).T.astype(BF)
    for place, item in enumerate((key, value_t, query, grad_t, graph_grad)):
        for head in range(HEADS):
            heads_ref[head, place * HD : (place + 1) * HD, :] = item[head * HD : (head + 1) * HD]


def list_kernel(mask_ref, list_ref, count_ref):
    def row(i, n):
        for j in range(NB):
            list_ref[n] = i * NB + j
            n = n + mask_ref[0, i, j]
        return n

    n = lax.fori_loop(0, NB, row, jnp.int32(0))
    for u in range(UNROLL):
        list_ref[n + u] = NB * NB
    count_ref[0] = n


def attention_kernel(
    list_ref, count_ref, x_ref, att_ref, grad_ref, keys, duo, expo, gprob, peak, top, total, inner,
    out_acc, q_acc, k_acc, v_acc,
):
    steps = lax.div(count_ref[0] + (UNROLL - 1), jnp.int32(UNROLL))
    duo[...] = jnp.zeros_like(duo)
    k_acc[...] = jnp.zeros_like(k_acc)
    v_acc[...] = jnp.zeros_like(v_acc)
    for b in range(NB):
        keys[b] = x_ref[b, 0:64, :].T
        duo[b, 0:HD, 0:BLK] = x_ref[b, 64:96, :]
        duo[b, HD : 2 * HD, BLK : 2 * BLK] = x_ref[b, 96:128, :]

    def pair(step, u):
        p = step * UNROLL + u
        index = list_ref[p]
        return p, lax.shift_right_logical(index, 4), lax.bitwise_and(index, 15)

    def scores(step, carry):
        before, m, l, d = carry
        parts = []
        for u in range(UNROLL):
            p, i, j = pair(step, u)
            both = jnp.dot(keys[j], duo[i], preferred_element_type=F32)
            s = both[:, :BLK]
            parts.append((p, i, s, both[:, BLK:], jnp.max(s, axis=0, keepdims=True)))
        for p, i, s, g, high in parts:
            same = i == before
            m_old = jnp.where(same, m, LOWEST)
            m = jnp.maximum(m_old, high)
            fade = jnp.exp2((m_old - m) * EXP_SCALE)
            e = jnp.exp2((s - m) * EXP_SCALE)
            l = jnp.where(same, l, 0.0) * fade + jnp.sum(e, axis=0, keepdims=True)
            d = jnp.where(same, d, 0.0) * fade + jnp.sum(e * g, axis=0, keepdims=True)
            expo[p] = e
            gprob[p] = g
            peak[p] = m
            top[i] = m
            total[i] = l
            inner[i] = d
            before = i
        return before, m, l, d

    zero = jnp.zeros((1, BLK), F32)
    lax.fori_loop(0, steps, scores, (jnp.int32(-1), zero, zero, zero))

    def grads(step, carry):
        before, o, q = carry
        for u in range(UNROLL):
            p, i, j = pair(step, u)
            share = 1.0 / total[i]
            prob = expo[p] * (jnp.exp2((peak[p] - top[i]) * EXP_SCALE) * share)
            low = prob.astype(BF)
            ds = (prob * (gprob[p] - inner[i] * share) * SCALE).astype(BF)
            same = i == before
            o = jnp.where(same, o, 0.0) + jnp.dot(
                x_ref[j, 32:64, :], low, preferred_element_type=F32
            )
            q = jnp.where(same, q, 0.0) + jnp.dot(
                x_ref[j, 0:32, :], ds, preferred_element_type=F32
            )
            out_acc[i] = o
            q_acc[i] = q
            k_acc[j] += lax.dot_general(
                duo[i, 0:HD, 0:BLK], ds, (((1,), (1,)), ((), ())), preferred_element_type=F32
            )
            v_acc[j] += lax.dot_general(
                duo[i, HD : 2 * HD, BLK : 2 * BLK], low, (((1,), (1,)), ((), ())),
                preferred_element_type=F32,
            )
            before = i
        return before, o, q

    wide = jnp.zeros((HD, BLK), F32)
    lax.fori_loop(0, steps, grads, (jnp.int32(-1), wide, wide))

    for b in range(NB):
        cols = slice(b * BLK, (b + 1) * BLK)
        att_ref[b] = out_acc[b].astype(BF)
        grad_ref[0:32, cols] = q_acc[b].astype(BF)
        grad_ref[32:64, cols] = k_acc[b].astype(BF)
        grad_ref[64:96, cols] = (
            v_acc[b].astype(BF).astype(F32) + x_ref[b, 128:160, :].astype(F32)
        ).astype(BF)


def weights_kernel(place_ref, grad_ref, masked_ref, keep_ref, send_ref):
    core = lax.bitwise_and(place_ref[0], 1)
    both = jnp.dot(
        grad_ref[...], masked_ref[...].reshape(NB * ROWS, WIDTH), preferred_element_type=F32
    )
    for half, first in ((0, True), (1, False)):
        for lane in range(2):
            for r in range(8):
                piece = both[
                    r * CHUNK : (r + 1) * CHUNK,
                    (half * 2 + lane) * 128 : (half * 2 + lane + 1) * 128,
                ]
                slot = lane * 8 + r

                @pl.when(core == half)
                def _():
                    keep_ref[slot] = piece

                @pl.when(core != half)
                def _():
                    send_ref[slot] = piece


def output_kernel(place_ref, own_ref, other_ref, q_ref, k_ref, v_ref, full):
    core = lax.bitwise_and(place_ref[0], 1)
    for half in range(2):
        mine = core == half
        for lane in range(2):
            for r in range(8):
                slot = lane * 8 + r
                full[
                    r * CHUNK : (r + 1) * CHUNK,
                    (half * 2 + lane) * 128 : (half * 2 + lane + 1) * 128,
                ] = jnp.where(mine, own_ref[slot], other_ref[slot])
    for lane in range(4):
        block = full[:, lane * 128 : (lane + 1) * 128].T
        for place, ref in enumerate((q_ref, k_ref, v_ref)):
            ref[lane * 128 : (lane + 1) * 128, :] = block[:, place * HD : (place + 1) * HD]


def mixed_kernel(
    place_ref, counts_ref, targets_ref, att_ref, local_ref, degree_ref, lower_ref, upper_ref,
    mixed_ref,
):
    border = jnp.zeros((ROWS, WIDTH), F32)
    for side, ref in ((0, lower_ref), (1, upper_ref)):
        here = attach(targets_ref[0, side : side + 1, :], counts_ref, place_ref, side)
        border = border + jnp.dot(here.astype(BF), ref[0], preferred_element_type=F32)
    graph = (local_ref[...] + border) / degree_ref[...]
    attended = att_ref[...].reshape(WIDTH, ROWS).astype(F32).T
    mixed_ref[0] = (attended + graph).astype(BF)


def call(kernel, name, shapes, in_specs, scratch=(), limit=32, flops=0, moved=0):
    out = tuple(jax.ShapeDtypeStruct(shape, kind) for shape, kind in shapes)
    return pl.pallas_call(
        kernel,
        out_shape=out,
        in_specs=in_specs,
        out_specs=tuple(VM for _ in out),
        scratch_shapes=scratch,
        compiler_params=pltpu.CompilerParams(vmem_limit_bytes=limit * 1024 * 1024),
        cost_estimate=pl.CostEstimate(flops=flops, bytes_accessed=moved, transcendentals=0),
        name=name,
    )


def on_device(
    features, mask_token, w_query, w_key, w_value, block_mask, masked_ids, adjacency, boundary_ids,
    boundary_counts, boundary_targets, grad_out,
):
    clusters = lax.axis_size("dp")
    place = jnp.stack(
        [lax.axis_index("dp"), lax.axis_index("seq"), jnp.int32(clusters)]
    ).astype(jnp.int32)

    masked, heads, outgoing, local, degree = call(
        rows_kernel,
        "rows",
        [
            ((ROWS, WIDTH), BF),
            ((HEADS, 5 * HD, ROWS), BF),
            ((2, 32, WIDTH), BF),
            ((ROWS, WIDTH), F32),
            ((ROWS, 1), F32),
        ],
        [SM, SM] + [VM] * 10,
        flops=400_000_000,
        moved=3_000_000,
    )(
        place, boundary_counts, features, mask_token[None], w_query, w_key, w_value, masked_ids,
        adjacency, boundary_ids, boundary_targets, grad_out,
    )

    x = lax.all_to_all(heads, "seq", split_axis=0, concat_axis=0, tiled=True)
    spread = jnp.broadcast_to(masked[None], (NB, ROWS, WIDTH))
    masked_all = lax.all_to_all(spread, "seq", split_axis=0, concat_axis=0, tiled=True)
    up = [(c, c + 1) for c in range(clusters - 1)]
    lower = lax.ppermute(outgoing[0:1], "dp", up)
    upper = lax.ppermute(outgoing[1:2], "dp", [(b, a) for a, b in up])

    pairs, count = pl.pallas_call(
        list_kernel,
        out_shape=(
            jax.ShapeDtypeStruct((SLOTS + 4,), jnp.int32),
            jax.ShapeDtypeStruct((1,), jnp.int32),
        ),
        in_specs=[SM],
        out_specs=(SM, SM),
        cost_estimate=pl.CostEstimate(flops=1_000_000, bytes_accessed=2_000_000, transcendentals=0),
        name="pair_list",
    )(block_mask)

    attended, grads = call(
        attention_kernel,
        "attention",
        [((NB, HD, BLK), BF), ((3 * HD, NB * BLK), BF)],
        [SM, SM, VM],
        scratch=[
            pltpu.VMEM((NB, BLK, 2 * HD), BF),
            pltpu.VMEM((NB + 1, 2 * HD, 2 * BLK), BF),
            pltpu.VMEM((SLOTS, BLK, BLK), F32),
            pltpu.VMEM((SLOTS, BLK, BLK), F32),
            pltpu.VMEM((SLOTS, 1, BLK), F32),
            pltpu.VMEM((NB + 1, 1, BLK), F32),
            pltpu.VMEM((NB + 1, 1, BLK), F32),
            pltpu.VMEM((NB + 1, 1, BLK), F32),
            pltpu.VMEM((NB + 1, HD, BLK), F32),
            pltpu.VMEM((NB + 1, HD, BLK), F32),
            pltpu.VMEM((NB, HD, BLK), F32),
            pltpu.VMEM((NB, HD, BLK), F32),
        ],
        limit=48,
        flops=5_000_000_000,
        moved=20_000_000,
    )(pairs, count, x)

    back = lax.all_to_all(attended, "seq", split_axis=0, concat_axis=0, tiled=True)
    (mixed,) = call(
        mixed_kernel,
        "mixed",
        [((1, ROWS, WIDTH), BF)],
        [SM, SM] + [VM] * 6,
        flops=20_000_000,
        moved=1_000_000,
    )(place, boundary_counts, boundary_targets, back, local, degree, lower, upper)

    keep, send = call(
        weights_kernel,
        "weights",
        [((CHIPS, CHUNK, 128), F32), ((CHIPS, CHUNK, 128), F32)],
        [SM, VM, VM],
        flops=200_000_000,
        moved=3_000_000,
    )(place, grads, masked_all)

    swap = [(c, c ^ 1) for c in range(clusters)]
    groups = [[chip * 2 + core for chip in range(clusters // 2)] for core in range(2)]
    pair_sum = keep + lax.ppermute(send, "dp", swap)
    terms = lax.all_to_all(
        pair_sum, "dp", split_axis=0, concat_axis=0, tiled=True, axis_index_groups=groups
    )
    reduced = jnp.broadcast_to(jnp.sum(terms, axis=0, keepdims=True), terms.shape)
    half = lax.all_to_all(
        reduced, "dp", split_axis=0, concat_axis=0, tiled=True, axis_index_groups=groups
    )
    other = lax.ppermute(half, "dp", swap)
    grad_query, grad_key, grad_value = call(
        output_kernel,
        "outputs",
        [((WIDTH, HD), F32)] * 3,
        [SM, VM, VM],
        scratch=[pltpu.VMEM((3 * HD, WIDTH), F32)],
        flops=1_000_000,
        moved=1_000_000,
    )(place, half, other)
    return mixed, grad_query, grad_key, grad_value


def solution(mesh):
    placed = (
        P("dp", "seq", None),
        P(),
        P(),
        P(),
        P(),
        P("dp", None, None),
        P("dp", None),
        P("dp", "seq", None),
        P("dp", None, "seq"),
        P("dp", None, "seq"),
        P("dp", None, "seq"),
        P("dp", "seq", None),
    )
    return jax.shard_map(
        on_device,
        mesh=mesh,
        in_specs=placed,
        out_specs=(P("dp", "seq", None), P(None, "seq"), P(None, "seq"), P(None, "seq")),
        check_vma=False,
    )
```

```python
import jax
import jax.numpy as jnp
from jax import lax
from jax.experimental import pallas as pl
from jax.experimental.pallas import tpu as pltpu
from jax.sharding import PartitionSpec as P

HEADS = 16
NB = 16
BLK = 128
HD = 32
ROWS = 128
WIDTH = 512
UNROLL = 4
SLOTS = NB * NB + UNROLL
SCALE = HD**-0.5
LOG2E = 1.4426950408889634
EXP_SCALE = SCALE * LOG2E
LOWEST = -3e38
BF = jnp.bfloat16
F32 = jnp.float32
CHIPS = 16
CHUNK = 12

SM = pl.BlockSpec(memory_space=pltpu.SMEM)
VM = pl.BlockSpec(memory_space=pltpu.VMEM)


def attach(targets, counts, side):
    slots = targets.shape[1]
    rows = lax.broadcasted_iota(jnp.int32, (ROWS, slots), 0)
    slot = lax.broadcasted_iota(jnp.int32, (ROWS, slots), 1)
    place = lax.axis_index("dp")
    inside = (place > 0) if side == 0 else (place < lax.axis_size("dp") - 1)
    limit = jnp.where(inside, counts, 0)
    return jnp.where((targets == rows) & (slot < limit), 1.0, 0.0)


def rows_kernel(*refs):
    sources, refs = refs[:11], refs[11:]
    masked_ref, heads_ref, lower_ref, upper_ref, local_ref, degree_ref, pick_ref = refs[:7]
    holds, sems = refs[7:18], refs[18]
    copies = [
        pltpu.make_async_copy(source, hold, sems.at[n])
        for n, (source, hold) in enumerate(zip(sources, holds))
    ]
    for copy in copies:
        copy.start()
    (
        ids_ref, counts_ref, token_ref, tokens_ref, wv_ref, links_ref, sends_ref, targets_ref,
        grad_ref, wk_ref, wq_ref,
    ) = holds
    for copy in copies[:5]:
        copy.wait()
    own = lax.axis_index("seq") * ROWS + lax.broadcasted_iota(jnp.int32, (ROWS, 128), 0)
    hit = own < 0
    for part in range(ids_ref.shape[1] // 128):
        hit = hit | (own == ids_ref[:, part * 128 : (part + 1) * 128])
    marked = jnp.max(jnp.where(hit, 1.0, 0.0), axis=1, keepdims=True) > 0
    masked = jnp.where(marked, token_ref[...].reshape(1, WIDTH).astype(F32), tokens_ref[0].astype(F32)).astype(BF)
    for lane in range(4):
        masked_ref[lane * 128 : (lane + 1) * 128, :] = masked[:, lane * 128 : (lane + 1) * 128]

    value_wide = jnp.dot(masked, wv_ref[...], preferred_element_type=F32)
    value = value_wide.astype(BF)
    for copy in copies[5:]:
        copy.wait()
    links_low = links_ref[0].astype(F32).astype(BF)
    local_ref[...] = value.astype(F32) + jnp.dot(links_low, value, preferred_element_type=F32)
    slots = sends_ref.shape[2]
    rows = lax.broadcasted_iota(jnp.int32, (ROWS, slots), 0)
    for side, ref in ((0, lower_ref), (1, upper_ref)):
        onehot = jnp.where(sends_ref[0, side : side + 1, :] == rows, 1.0, 0.0).astype(BF)
        ref[0] = lax.dot_general(
            onehot, value, (((0,), (0,)), ((), ())), preferred_element_type=F32
        ).astype(BF)

    degree = 1.0 + jnp.sum(links_ref[0].astype(F32), axis=1, keepdims=True)
    for side in range(2):
        here = attach(
            targets_ref[0, side : side + 1, :], counts_ref[0, :, side : side + 1], side
        )
        pick_ref[:, side * slots : (side + 1) * slots] = here.astype(BF)
        degree = degree + jnp.sum(here, axis=1, keepdims=True)
    degree_ref[...] = degree

    scaled = (grad_ref[0].astype(F32) / degree).T
    high = scaled.astype(BF)
    rest = scaled - high.astype(F32)
    mid = rest.astype(BF)
    low = (rest - mid.astype(F32)).astype(BF)
    spread = jnp.dot(low, links_low, preferred_element_type=F32)
    spread = spread + jnp.dot(mid, links_low, preferred_element_type=F32)
    spread = spread + jnp.dot(high, links_low, preferred_element_type=F32)
    graph_grad = (scaled + spread).astype(BF)

    key = jnp.dot(masked, wk_ref[...], preferred_element_type=F32).T.astype(BF)
    query = jnp.dot(masked, wq_ref[...], preferred_element_type=F32).T.astype(BF)
    value_t = value_wide.T.astype(BF)
    grad_t = grad_ref[0].astype(F32).T.astype(BF)
    for place, item in enumerate((key, value_t, query, grad_t, graph_grad)):
        for head in range(HEADS):
            heads_ref[head, place * HD : (place + 1) * HD, :] = item[head * HD : (head + 1) * HD]


def attention_kernel(
    mask_ref, x_ref, masked_ref, back_ref, grad_ref, list_ref, keys, duo, expo, gprob, peak, top, total, inner,
    out_acc, q_acc, k_acc, v_acc,
):
    count = jnp.int32(0)
    for i in range(NB):
        for j in range(NB):
            list_ref[count] = i * NB + j
            count = count + mask_ref[0, i, j]
    for u in range(UNROLL):
        list_ref[count + u] = NB * NB
    steps = lax.div(count + (UNROLL - 1), jnp.int32(UNROLL))
    duo[...] = jnp.zeros_like(duo)
    k_acc[...] = jnp.zeros_like(k_acc)
    v_acc[...] = jnp.zeros_like(v_acc)
    for b in range(NB):
        keys[b] = x_ref[b, 0:64, :].T
        duo[b, 0:HD, 0:BLK] = x_ref[b, 64:96, :]
        duo[b, HD : 2 * HD, BLK : 2 * BLK] = x_ref[b, 96:128, :]

    def pair(step, u):
        p = step * UNROLL + u
        index = list_ref[p]
        return p, lax.shift_right_logical(index, 4), lax.bitwise_and(index, 15)

    def scores(step, carry):
        before, m, l, d = carry
        parts = []
        for u in range(UNROLL):
            p, i, j = pair(step, u)
            both = jnp.dot(keys[j], duo[i], preferred_element_type=F32)
            s = both[:, :BLK]
            parts.append((p, i, s, both[:, BLK:], jnp.max(s, axis=0, keepdims=True)))
        for p, i, s, g, high in parts:
            same = i == before
            m_old = jnp.where(same, m, LOWEST)
            m = jnp.maximum(m_old, high)
            fade = jnp.exp2((m_old - m) * EXP_SCALE)
            e = jnp.exp2((s - m) * EXP_SCALE)
            l = jnp.where(same, l, 0.0) * fade + jnp.sum(e, axis=0, keepdims=True)
            d = jnp.where(same, d, 0.0) * fade + jnp.sum(e * g, axis=0, keepdims=True)
            expo[p] = e
            gprob[p] = g
            peak[p] = m
            top[i] = m
            total[i] = l
            inner[i] = d
            before = i
        return before, m, l, d

    zero = jnp.zeros((1, BLK), F32)
    lax.fori_loop(0, steps, scores, (jnp.int32(-1), zero, zero, zero))

    def grads(step, carry):
        before, o, q = carry
        for u in range(UNROLL):
            p, i, j = pair(step, u)
            share = 1.0 / total[i]
            prob = expo[p] * (jnp.exp2((peak[p] - top[i]) * EXP_SCALE) * share)
            low = prob.astype(BF)
            ds = (prob * (gprob[p] - inner[i] * share) * SCALE).astype(BF)
            same = i == before
            o = jnp.where(same, o, 0.0) + jnp.dot(
                x_ref[j, 32:64, :], low, preferred_element_type=F32
            )
            q = jnp.where(same, q, 0.0) + jnp.dot(
                x_ref[j, 0:32, :], ds, preferred_element_type=F32
            )
            out_acc[i] = o
            q_acc[i] = q
            k_acc[j] += lax.dot_general(
                duo[i, 0:HD, 0:BLK], ds, (((1,), (1,)), ((), ())), preferred_element_type=F32
            )
            v_acc[j] += lax.dot_general(
                duo[i, HD : 2 * HD, BLK : 2 * BLK], low, (((1,), (1,)), ((), ())),
                preferred_element_type=F32,
            )
            before = i
        return before, o, q

    wide = jnp.zeros((HD, BLK), F32)
    lax.fori_loop(0, steps, grads, (jnp.int32(-1), wide, wide))

    for b in range(NB):
        cols = slice(b * BLK, (b + 1) * BLK)
        back_ref[b, 0:WIDTH, :] = masked_ref[...]
        back_ref[b, WIDTH : WIDTH + HD, :] = out_acc[b].astype(BF)
        grad_ref[0:32, cols] = q_acc[b].astype(BF)
        grad_ref[32:64, cols] = k_acc[b].astype(BF)
        grad_ref[64:96, cols] = (
            v_acc[b].astype(BF).astype(F32) + x_ref[b, 128:160, :].astype(F32)
        ).astype(BF)


def weights_kernel(grad_ref, masked_ref, keep_ref, send_ref, att_ref):
    core = lax.bitwise_and(lax.axis_index("dp"), 1)
    masked = jnp.concatenate(
        [
            jnp.concatenate(
                [masked_ref[b, lane * 128 : (lane + 1) * 128, :] for b in range(NB)], axis=0
            )
            for lane in range(4)
        ],
        axis=1,
    )
    both = jnp.dot(grad_ref[...], masked, preferred_element_type=F32)
    for head in range(HEADS):
        att_ref[head * HD : (head + 1) * HD, :] = masked_ref[head, WIDTH : WIDTH + HD, :]
    own_low = core == 0
    for lane in range(2):
        low = both[:, lane * 128 : (lane + 1) * 128]
        high = both[:, (lane + 2) * 128 : (lane + 3) * 128]
        keep = jnp.where(own_low, low, high)
        send = jnp.where(own_low, high, low)
        for r in range(8):
            keep_ref[lane * 8 + r] = keep[r * CHUNK : (r + 1) * CHUNK]
            send_ref[lane * 8 + r] = send[r * CHUNK : (r + 1) * CHUNK]


def output_kernel(own_ref, other_ref, q_ref, k_ref, v_ref, full):
    own_low = lax.bitwise_and(lax.axis_index("dp"), 1) == 0
    for lane in range(2):
        for r in range(8):
            own = own_ref[lane * 8 + r]
            other = other_ref[lane * 8 + r]
            rows = slice(r * CHUNK, (r + 1) * CHUNK)
            full[rows, lane * 128 : (lane + 1) * 128] = jnp.where(own_low, own, other)
            full[rows, (lane + 2) * 128 : (lane + 3) * 128] = jnp.where(own_low, other, own)
    for place, ref in enumerate((q_ref, k_ref, v_ref)):
        ref[...] = full[place * HD : (place + 1) * HD, :]


def mixed_kernel(pick_ref, att_ref, local_ref, degree_ref, lower_ref, upper_ref, mixed_ref):
    rows = jnp.concatenate([lower_ref[0], upper_ref[0]], axis=0)
    border = jnp.dot(pick_ref[...], rows, preferred_element_type=F32)
    graph = (local_ref[...] + border) / degree_ref[...]
    attended = att_ref[...].astype(F32).T
    mixed_ref[0] = (attended + graph).astype(BF)


def call(kernel, name, shapes, in_specs, scratch=(), limit=32, flops=0, moved=0):
    out = tuple(jax.ShapeDtypeStruct(shape, kind) for shape, kind in shapes)
    return pl.pallas_call(
        kernel,
        out_shape=out,
        in_specs=in_specs,
        out_specs=tuple(VM for _ in out),
        scratch_shapes=scratch,
        compiler_params=pltpu.CompilerParams(vmem_limit_bytes=limit * 1024 * 1024),
        cost_estimate=pl.CostEstimate(flops=flops, bytes_accessed=moved, transcendentals=0),
        name=name,
    )


def on_device(
    features, mask_token, w_query, w_key, w_value, block_mask, masked_ids, adjacency, boundary_ids,
    boundary_counts, boundary_targets, grad_out,
):
    clusters = lax.axis_size("dp")
    slots = boundary_ids.shape[2]
    sources = (
        masked_ids, boundary_counts.transpose(0, 2, 1), mask_token, features, w_value,
        adjacency, boundary_ids, boundary_targets, grad_out, w_key, w_query,
    )
    masked, heads, send_lower, send_upper, local, degree, pick = call(
        rows_kernel,
        "rows",
        [
            ((WIDTH, ROWS), BF),
            ((HEADS, 5 * HD, ROWS), BF),
            ((1, slots, WIDTH), BF),
            ((1, slots, WIDTH), BF),
            ((ROWS, WIDTH), F32),
            ((ROWS, 1), F32),
            ((ROWS, 2 * slots), BF),
        ],
        [pl.BlockSpec(memory_space=pltpu.HBM)] * len(sources),
        scratch=[pltpu.VMEM(item.shape, item.dtype) for item in sources]
        + [pltpu.SemaphoreType.DMA((len(sources),))],
        flops=400_000_000,
        moved=3_000_000,
    )(*[pltpu.with_memory_space_constraint(item, pltpu.HBM) for item in sources])

    x = lax.all_to_all(heads, "seq", split_axis=0, concat_axis=0, tiled=True)
    up = [(c, c + 1) for c in range(clusters - 1)]
    lower = lax.ppermute(send_lower, "dp", up)
    upper = lax.ppermute(send_upper, "dp", [(b, a) for a, b in up])

    back, grads = call(
        attention_kernel,
        "attention",
        [((NB, WIDTH + HD, BLK), BF), ((3 * HD, NB * BLK), BF)],
        [SM, VM, VM],
        scratch=[
            pltpu.SMEM((SLOTS + UNROLL,), jnp.int32),
            pltpu.VMEM((NB, BLK, 2 * HD), BF),
            pltpu.VMEM((NB + 1, 2 * HD, 2 * BLK), BF),
            pltpu.VMEM((SLOTS, BLK, BLK), F32),
            pltpu.VMEM((SLOTS, BLK, BLK), F32),
            pltpu.VMEM((SLOTS, 1, BLK), F32),
            pltpu.VMEM((NB + 1, 1, BLK), F32),
            pltpu.VMEM((NB + 1, 1, BLK), F32),
            pltpu.VMEM((NB + 1, 1, BLK), F32),
            pltpu.VMEM((NB + 1, HD, BLK), F32),
            pltpu.VMEM((NB + 1, HD, BLK), F32),
            pltpu.VMEM((NB, HD, BLK), F32),
            pltpu.VMEM((NB, HD, BLK), F32),
        ],
        limit=48,
        flops=5_000_000_000,
        moved=20_000_000,
    )(block_mask, x, masked)

    back = lax.all_to_all(back, "seq", split_axis=0, concat_axis=0, tiled=True)
    keep, send, attended = call(
        weights_kernel,
        "weights",
        [((CHIPS, CHUNK, 128), F32), ((CHIPS, CHUNK, 128), F32), ((WIDTH, ROWS), BF)],
        [VM, VM],
        flops=200_000_000,
        moved=3_000_000,
    )(grads, back)
    (mixed,) = call(
        mixed_kernel,
        "mixed",
        [((1, ROWS, WIDTH), BF)],
        [VM] * 6,
        flops=20_000_000,
        moved=1_000_000,
    )(pick, attended, local, degree, lower, upper)

    swap = [(c, c ^ 1) for c in range(clusters)]
    groups = [[chip * 2 + core for chip in range(clusters // 2)] for core in range(2)]
    pair_sum = keep + lax.ppermute(send, "dp", swap)
    terms = lax.all_to_all(
        pair_sum, "dp", split_axis=0, concat_axis=0, tiled=True, axis_index_groups=groups
    )
    reduced = jnp.broadcast_to(jnp.sum(terms, axis=0, keepdims=True), terms.shape)
    half = lax.all_to_all(
        reduced, "dp", split_axis=0, concat_axis=0, tiled=True, axis_index_groups=groups
    )
    other = lax.ppermute(half, "dp", swap)
    grad_query, grad_key, grad_value = call(
        output_kernel,
        "outputs",
        [((HD, WIDTH), F32)] * 3,
        [VM, VM],
        scratch=[pltpu.VMEM((3 * HD, WIDTH), F32)],
        flops=1_000_000,
        moved=1_000_000,
    )(half, other)
    return mixed, grad_query.T, grad_key.T, grad_value.T


def solution(mesh):
    placed = (
        P("dp", "seq", None),
        P(),
        P(),
        P(),
        P(),
        P("dp", None, None),
        P("dp", None),
        P("dp", "seq", None),
        P("dp", None, "seq"),
        P("dp", None, "seq"),
        P("dp", None, "seq"),
        P("dp", "seq", None),
    )
    return jax.shard_map(
        on_device,
        mesh=mesh,
        in_specs=placed,
        out_specs=(P("dp", "seq", None), P(None, "seq"), P(None, "seq"), P(None, "seq")),
        check_vma=False,
    )
```

```python
import jax
import jax.numpy as jnp
from jax import lax
from jax.experimental import pallas as pl
from jax.experimental.pallas import tpu as pltpu
from jax.sharding import PartitionSpec as P

HEADS = 16
NB = 16
BLK = 128
HD = 32
ROWS = 128
WIDTH = 512
UNROLL = 16
SLOTS = NB * NB + UNROLL
SCALE = HD**-0.5
LOG2E = 1.4426950408889634
EXP_SCALE = SCALE * LOG2E
LOWEST = -3e38
BF = jnp.bfloat16
F32 = jnp.float32
NEAR = 4
CHUNK = 48

SM = pl.BlockSpec(memory_space=pltpu.SMEM)
VM = pl.BlockSpec(memory_space=pltpu.VMEM)
ANY = pl.BlockSpec(memory_space=pl.ANY)


def group_of(place):
    return (place // 4 % 2) * 2 + place % 2


def attach(targets, counts, side):
    slots = targets.shape[1]
    rows = lax.broadcasted_iota(jnp.int32, (ROWS, slots), 0)
    slot = lax.broadcasted_iota(jnp.int32, (ROWS, slots), 1)
    place = lax.axis_index("dp")
    inside = (place > 0) if side == 0 else (place < lax.axis_size("dp") - 1)
    limit = jnp.where(inside, counts, 0)
    return jnp.where((targets == rows) & (slot < limit), 1.0, 0.0)


def rows_kernel(*refs):
    sources, refs = refs[:11], refs[11:]
    heads_ref, lower_ref, upper_ref, local_ref, degree_ref, pick_ref = refs[:6]
    holds, sems = refs[6:17], refs[17]
    copies = [
        pltpu.make_async_copy(source, hold, sems.at[n])
        for n, (source, hold) in enumerate(zip(sources, holds))
    ]
    for copy in copies:
        copy.start()
    (
        ids_ref, counts_ref, token_ref, tokens_ref, wv_ref, links_ref, sends_ref, targets_ref,
        grad_ref, wk_ref, wq_ref,
    ) = holds
    for copy in copies[:5]:
        copy.wait()
    own = lax.axis_index("seq") * ROWS + lax.broadcasted_iota(jnp.int32, (ROWS, 128), 0)
    hit = own < 0
    for part in range(ids_ref.shape[1] // 128):
        hit = hit | (own == ids_ref[:, part * 128 : (part + 1) * 128])
    marked = jnp.max(jnp.where(hit, 1.0, 0.0), axis=1, keepdims=True) > 0
    masked = jnp.where(marked, token_ref[...].reshape(1, WIDTH).astype(F32), tokens_ref[0].astype(F32)).astype(BF)
    for head in range(HEADS):
        group = group_of(head)
        heads_ref[head, 0:BLK, :] = masked[:, group * 128 : (group + 1) * 128]

    value_wide = jnp.dot(masked, wv_ref[...], preferred_element_type=F32)
    value = value_wide.astype(BF)
    for copy in copies[5:]:
        copy.wait()
    links_low = links_ref[0].astype(F32).astype(BF)
    local_ref[...] = value.astype(F32) + jnp.dot(links_low, value, preferred_element_type=F32)
    slots = sends_ref.shape[2]
    rows = lax.broadcasted_iota(jnp.int32, (ROWS, slots), 0)
    for side, ref in ((0, lower_ref), (1, upper_ref)):
        onehot = jnp.where(sends_ref[0, side : side + 1, :] == rows, 1.0, 0.0).astype(BF)
        ref[0] = lax.dot_general(
            onehot, value, (((0,), (0,)), ((), ())), preferred_element_type=F32
        ).astype(BF)

    degree = 1.0 + jnp.sum(links_ref[0].astype(F32), axis=1, keepdims=True)
    for side in range(2):
        here = attach(
            targets_ref[0, side : side + 1, :], counts_ref[0, :, side : side + 1], side
        )
        pick_ref[:, side * slots : (side + 1) * slots] = here.astype(BF)
        degree = degree + jnp.sum(here, axis=1, keepdims=True)
    degree_ref[...] = degree

    scaled = (grad_ref[0].astype(F32) / degree).T
    high = scaled.astype(BF)
    rest = scaled - high.astype(F32)
    mid = rest.astype(BF)
    low = (rest - mid.astype(F32)).astype(BF)
    spread = jnp.dot(low, links_low, preferred_element_type=F32)
    spread = spread + jnp.dot(mid, links_low, preferred_element_type=F32)
    spread = spread + jnp.dot(high, links_low, preferred_element_type=F32)
    graph_grad = (scaled + spread).astype(BF)

    key = jnp.dot(masked, wk_ref[...], preferred_element_type=F32).T.astype(BF)
    query = jnp.dot(masked, wq_ref[...], preferred_element_type=F32).T.astype(BF)
    value_t = value_wide.T.astype(BF)
    grad_t = grad_ref[0].astype(F32).T.astype(BF)
    for place, item in enumerate((key, value_t, query, grad_t, graph_grad)):
        for head in range(HEADS):
            heads_ref[head, BLK + place * HD : BLK + (place + 1) * HD, :] = item[
                head * HD : (head + 1) * HD
            ]


def columns_kernel(graph_ref, x_ref, columns_ref):
    columns_ref[...] = x_ref[:, 0:BLK, :]


def attention_kernel(
    mask_ref, x_ref, back_ref, grad_ref, list_ref, keys, duo, expo, gprob, peak, top, total, inner,
    out_acc, q_acc, k_acc, v_acc,
):
    count = jnp.int32(0)
    for i in range(NB):
        for j in range(NB):
            list_ref[count] = i * NB + j
            count = count + mask_ref[0, i, j]
    for u in range(UNROLL):
        list_ref[count + u] = NB * NB
    steps = lax.div(count + (UNROLL - 1), jnp.int32(UNROLL))
    duo[...] = jnp.zeros_like(duo)
    k_acc[...] = jnp.zeros_like(k_acc)
    v_acc[...] = jnp.zeros_like(v_acc)
    for b in range(NB):
        keys[b] = x_ref[b, BLK : BLK + 64, :].T
        duo[b, 0:HD, 0:BLK] = x_ref[b, BLK + 64 : BLK + 96, :]
        duo[b, HD : 2 * HD, BLK : 2 * BLK] = x_ref[b, BLK + 96 : BLK + 128, :]

    def pair(step, u):
        p = step * UNROLL + u
        index = list_ref[p]
        return p, lax.shift_right_logical(index, 4), lax.bitwise_and(index, 15)

    def scores(step, carry):
        before, m, l, d = carry
        parts = []
        for u in range(UNROLL):
            p, i, j = pair(step, u)
            both = jnp.dot(keys[j], duo[i], preferred_element_type=F32)
            s = both[:, :BLK]
            parts.append((p, i, s, both[:, BLK:], jnp.max(s, axis=0, keepdims=True)))
        for p, i, s, g, high in parts:
            same = i == before
            m_old = jnp.where(same, m, LOWEST)
            m = jnp.maximum(m_old, high)
            fade = jnp.exp2((m_old - m) * EXP_SCALE)
            e = jnp.exp2((s - m) * EXP_SCALE)
            l = jnp.where(same, l, 0.0) * fade + jnp.sum(e, axis=0, keepdims=True)
            d = jnp.where(same, d, 0.0) * fade + jnp.sum(e * g, axis=0, keepdims=True)
            expo[p] = e
            gprob[p] = g
            peak[p] = m
            top[i] = m
            total[i] = l
            inner[i] = d
            before = i
        return before, m, l, d

    zero = jnp.zeros((1, BLK), F32)
    lax.fori_loop(0, steps, scores, (jnp.int32(-1), zero, zero, zero))

    def grads(step, carry):
        before, o, q = carry
        for u in range(UNROLL):
            p, i, j = pair(step, u)
            share = 1.0 / total[i]
            prob = expo[p] * (jnp.exp2((peak[p] - top[i]) * EXP_SCALE) * share)
            low = prob.astype(BF)
            ds = (prob * (gprob[p] - inner[i] * share) * SCALE).astype(BF)
            same = i == before
            o = jnp.where(same, o, 0.0) + jnp.dot(
                x_ref[j, BLK + 32 : BLK + 64, :], low, preferred_element_type=F32
            )
            q = jnp.where(same, q, 0.0) + jnp.dot(
                x_ref[j, BLK : BLK + 32, :], ds, preferred_element_type=F32
            )
            out_acc[i] = o
            q_acc[i] = q
            k_acc[j] += lax.dot_general(
                duo[i, 0:HD, 0:BLK], ds, (((1,), (1,)), ((), ())), preferred_element_type=F32
            )
            v_acc[j] += lax.dot_general(
                duo[i, HD : 2 * HD, BLK : 2 * BLK], low, (((1,), (1,)), ((), ())),
                preferred_element_type=F32,
            )
            before = i
        return before, o, q

    wide = jnp.zeros((HD, BLK), F32)
    lax.fori_loop(0, steps, grads, (jnp.int32(-1), wide, wide))

    for b in range(NB):
        cols = slice(b * BLK, (b + 1) * BLK)
        back_ref[b] = out_acc[b].astype(BF)
        grad_ref[0:32, cols] = q_acc[b].astype(BF)
        grad_ref[32:64, cols] = k_acc[b].astype(BF)
        grad_ref[64:96, cols] = (
            v_acc[b].astype(BF).astype(F32) + x_ref[b, BLK + 128 : BLK + 160, :].astype(F32)
        ).astype(BF)


def weights_kernel(
    grad_ref, own_ref, down_ref, right_ref, far_ref, part_ref, full,
):
    group = group_of(lax.axis_index("seq"))
    pairs = (((own_ref, 0), (down_ref, 2)), ((right_ref, 1), (far_ref, 3)))
    for pair in pairs:
        columns = [ref[...].reshape(NB * ROWS, 128) for ref, _ in pair]
        both = jnp.dot(
            grad_ref[...], jnp.concatenate(columns, axis=1), preferred_element_type=F32
        )
        for n, (_, flip) in enumerate(pair):
            full[lax.bitwise_xor(group, flip)] = both[:, n * 128 : (n + 1) * 128]
    for lane in range(4):
        for half in range(2):
            part_ref[lane * 2 + half] = full[lane, half * CHUNK : (half + 1) * CHUNK, :]


def chip_kernel(back_ref, both_ref, sum_ref):
    start = lax.bitwise_and(lax.axis_index("dp"), 1) * NEAR
    sum_ref[...] = both_ref[pl.ds(start, NEAR)] + both_ref[pl.ds(2 * NEAR + start, NEAR)]


def output_kernel(all_ref, q_ref, k_ref, v_ref, full):
    for lane in range(4):
        for half in range(2):
            rows = slice(half * CHUNK, (half + 1) * CHUNK)
            full[rows, lane * 128 : (lane + 1) * 128] = all_ref[lane * 2 + half]
    for place, ref in enumerate((q_ref, k_ref, v_ref)):
        ref[...] = full[place * HD : (place + 1) * HD, :]


def graph_kernel(pick_ref, local_ref, degree_ref, lower_ref, upper_ref, graph_ref):
    rows = jnp.concatenate([lower_ref[0], upper_ref[0]], axis=0)
    border = jnp.dot(pick_ref[...], rows, preferred_element_type=F32)
    graph_ref[...] = (local_ref[...] + border) / degree_ref[...]


def mixed_kernel(att_ref, graph_ref, mixed_ref):
    attended = att_ref[...].reshape(WIDTH, ROWS).astype(F32).T
    mixed_ref[0] = (attended + graph_ref[...]).astype(BF)


def call(kernel, name, shapes, in_specs, scratch=(), limit=16, flops=0, moved=0):
    out = tuple(jax.ShapeDtypeStruct(shape, kind) for shape, kind in shapes)
    return pl.pallas_call(
        kernel,
        out_shape=out,
        in_specs=in_specs,
        out_specs=tuple(VM for _ in out),
        scratch_shapes=scratch,
        compiler_params=pltpu.CompilerParams(vmem_limit_bytes=limit * 1024 * 1024),
        cost_estimate=pl.CostEstimate(flops=flops, bytes_accessed=moved, transcendentals=0),
        name=name,
    )


def on_device(
    features, mask_token, w_query, w_key, w_value, block_mask, masked_ids, adjacency, boundary_ids,
    boundary_counts, boundary_targets, grad_out,
):
    clusters = lax.axis_size("dp")
    slots = boundary_ids.shape[2]
    sources = (
        masked_ids, boundary_counts.transpose(0, 2, 1), mask_token, features, w_value,
        adjacency, boundary_ids, boundary_targets, grad_out, w_key, w_query,
    )
    heads, send_lower, send_upper, local, degree, pick = call(
        rows_kernel,
        "rows",
        [
            ((HEADS, BLK + 5 * HD, ROWS), BF),
            ((1, slots, WIDTH), BF),
            ((1, slots, WIDTH), BF),
            ((ROWS, WIDTH), F32),
            ((ROWS, 1), F32),
            ((ROWS, 2 * slots), BF),
        ],
        [pl.BlockSpec(memory_space=pltpu.HBM)] * len(sources),
        scratch=[pltpu.VMEM(item.shape, item.dtype) for item in sources]
        + [pltpu.SemaphoreType.DMA((len(sources),))],
        flops=400_000_000,
        moved=3_000_000,
    )(*[pltpu.with_memory_space_constraint(item, pltpu.HBM) for item in sources])

    x = lax.all_to_all(heads, "seq", split_axis=0, concat_axis=0, tiled=True)
    up = [(c, c + 1) for c in range(clusters - 1)]
    lower = lax.ppermute(send_lower, "dp", up)
    upper = lax.ppermute(send_upper, "dp", [(b, a) for a, b in up])
    (graph,) = call(
        graph_kernel,
        "graph",
        [((ROWS, WIDTH), F32)],
        [VM] * 5,
        flops=20_000_000,
        moved=1_000_000,
    )(pick, local, degree, lower, upper)
    (columns,) = call(
        columns_kernel,
        "columns",
        [((NB, BLK, 128), BF)],
        [ANY, VM],
        flops=100_000,
        moved=1_000_000,
    )(graph, x)

    def neighbour(down, right, odd):
        def turn(n):
            return ((n + odd) ^ 1) - odd

        return lax.ppermute(
            columns,
            "seq",
            [
                (4 * y + x, 4 * ((turn(y) if down else y) % 4) + (turn(x) if right else x) % 4)
                for y in range(4)
                for x in range(4)
            ],
        )

    parts = [columns, neighbour(1, 0, 0), neighbour(0, 1, 0), neighbour(1, 1, 1)]

    back, grads = call(
        attention_kernel,
        "attention",
        [((NB, HD, BLK), BF), ((3 * HD, NB * BLK), BF)],
        [SM, VM],
        scratch=[
            pltpu.SMEM((SLOTS + UNROLL,), jnp.int32),
            pltpu.VMEM((NB, BLK, 2 * HD), BF),
            pltpu.VMEM((NB + 1, 2 * HD, 2 * BLK), BF),
            pltpu.VMEM((SLOTS, BLK, BLK), F32),
            pltpu.VMEM((SLOTS, BLK, BLK), F32),
            pltpu.VMEM((SLOTS, 1, BLK), F32),
            pltpu.VMEM((NB + 1, 1, BLK), F32),
            pltpu.VMEM((NB + 1, 1, BLK), F32),
            pltpu.VMEM((NB + 1, 1, BLK), F32),
            pltpu.VMEM((NB + 1, HD, BLK), F32),
            pltpu.VMEM((NB + 1, HD, BLK), F32),
            pltpu.VMEM((NB, HD, BLK), F32),
            pltpu.VMEM((NB, HD, BLK), F32),
        ],
        limit=44,
        flops=5_000_000_000,
        moved=20_000_000,
    )(block_mask, x)

    back = lax.all_to_all(back, "seq", split_axis=0, concat_axis=0, tiled=True)
    (part,) = call(
        weights_kernel,
        "weights",
        [((2 * NEAR, CHUNK, 128), F32)],
        [VM] * 5,
        scratch=[pltpu.VMEM((4, 3 * HD, 128), F32)],
        flops=200_000_000,
        moved=3_000_000,
    )(grads, *parts)
    (mixed,) = call(
        mixed_kernel,
        "mixed",
        [((1, ROWS, WIDTH), BF)],
        [VM, VM],
        flops=20_000_000,
        moved=1_000_000,
    )(back, graph)

    cores = [[c, c + 1] for c in range(0, clusters, 2)]
    span = 2 * NEAR
    near = [
        [g * span + 2 * n + core for n in range(NEAR)]
        for g in range(clusters // span)
        for core in range(2)
    ]
    far = [[g * span + n for g in range(clusters // span)] for n in range(span)]

    def exchange(item, groups):
        return lax.all_to_all(
            item, "dp", split_axis=0, concat_axis=0, tiled=True, axis_index_groups=groups
        )

    def gather(item, groups):
        return lax.all_gather(item, "dp", axis=0, tiled=True, axis_index_groups=groups)

    def copies(item, count):
        return jnp.broadcast_to(jnp.sum(item, axis=0, keepdims=True), (count,) + item.shape[1:])

    (chip_sum,) = call(
        chip_kernel,
        "chip_sum",
        [((NEAR, CHUNK, 128), F32)],
        [ANY, VM],
        flops=100_000,
        moved=300_000,
    )(back, gather(part, cores))
    terms = exchange(chip_sum, near)
    terms = exchange(copies(terms, clusters // span), far)
    reduced = gather(exchange(copies(terms, NEAR), near), cores)
    grad_query, grad_key, grad_value = call(
        output_kernel,
        "outputs",
        [((HD, WIDTH), F32)] * 3,
        [VM],
        scratch=[pltpu.VMEM((3 * HD, WIDTH), F32)],
        flops=1_000_000,
        moved=1_000_000,
    )(reduced)
    return mixed, grad_query.T, grad_key.T, grad_value.T


def solution(mesh):
    placed = (
        P("dp", "seq", None),
        P(),
        P(),
        P(),
        P(),
        P("dp", None, None),
        P("dp", None),
        P("dp", "seq", None),
        P("dp", None, "seq"),
        P("dp", None, "seq"),
        P("dp", None, "seq"),
        P("dp", "seq", None),
    )
    return jax.shard_map(
        on_device,
        mesh=mesh,
        in_specs=placed,
        out_specs=(P("dp", "seq", None), P(None, "seq"), P(None, "seq"), P(None, "seq")),
        check_vma=False,
    )
```

```python
import jax
import jax.numpy as jnp
from jax import lax
from jax.experimental import pallas as pl
from jax.experimental.pallas import tpu as pltpu
from jax.sharding import PartitionSpec as P

HEADS = 16
NB = 16
BLK = 128
HD = 32
ROWS = 128
WIDTH = 512
UNROLL = 16
SLOTS = NB * NB + UNROLL
SCALE = HD**-0.5
LOG2E = 1.4426950408889634
EXP_SCALE = SCALE * LOG2E
LOWEST = -3e38
BF = jnp.bfloat16
F32 = jnp.float32
NEAR = 4
CHUNK = 48

SM = pl.BlockSpec(memory_space=pltpu.SMEM)
VM = pl.BlockSpec(memory_space=pltpu.VMEM)
ANY = pl.BlockSpec(memory_space=pl.ANY)


def group_of(place):
    return (place // 4 % 2) * 2 + place % 2


def attach(targets, counts, side):
    slots = targets.shape[1]
    rows = lax.broadcasted_iota(jnp.int32, (ROWS, slots), 0)
    slot = lax.broadcasted_iota(jnp.int32, (ROWS, slots), 1)
    place = lax.axis_index("dp")
    inside = (place > 0) if side == 0 else (place < lax.axis_size("dp") - 1)
    limit = jnp.where(inside, counts, 0)
    return jnp.where((targets == rows) & (slot < limit), 1.0, 0.0)


def rows_kernel(*refs):
    sources, refs = refs[:11], refs[11:]
    heads_ref, lower_ref, upper_ref, local_ref, degree_ref, pick_ref = refs[:6]
    holds, sems = refs[6:17], refs[17]
    copies = [
        pltpu.make_async_copy(source, hold, sems.at[n])
        for n, (source, hold) in enumerate(zip(sources, holds))
    ]
    for copy in copies:
        copy.start()
    (
        ids_ref, counts_ref, token_ref, tokens_ref, wv_ref, links_ref, sends_ref, targets_ref,
        grad_ref, wk_ref, wq_ref,
    ) = holds
    for copy in copies[:5]:
        copy.wait()
    own = lax.axis_index("seq") * ROWS + lax.broadcasted_iota(jnp.int32, (ROWS, 128), 0)
    hit = own < 0
    for part in range(ids_ref.shape[1] // 128):
        hit = hit | (own == ids_ref[:, part * 128 : (part + 1) * 128])
    marked = jnp.max(jnp.where(hit, 1.0, 0.0), axis=1, keepdims=True) > 0
    masked = jnp.where(marked, token_ref[...].reshape(1, WIDTH).astype(F32), tokens_ref[0].astype(F32)).astype(BF)
    for head in range(HEADS):
        group = group_of(head)
        heads_ref[head, 0:BLK, :] = masked[:, group * 128 : (group + 1) * 128]

    value_wide = jnp.dot(masked, wv_ref[...], preferred_element_type=F32)
    value = value_wide.astype(BF)
    for copy in copies[5:]:
        copy.wait()
    links_low = links_ref[0].astype(F32).astype(BF)
    local_ref[...] = value.astype(F32) + jnp.dot(links_low, value, preferred_element_type=F32)
    slots = sends_ref.shape[2]
    rows = lax.broadcasted_iota(jnp.int32, (ROWS, slots), 0)
    for side, ref in ((0, lower_ref), (1, upper_ref)):
        onehot = jnp.where(sends_ref[0, side : side + 1, :] == rows, 1.0, 0.0).astype(BF)
        ref[0] = lax.dot_general(
            onehot, value, (((0,), (0,)), ((), ())), preferred_element_type=F32
        ).astype(BF)

    degree = 1.0 + jnp.sum(links_ref[0].astype(F32), axis=1, keepdims=True)
    for side in range(2):
        here = attach(
            targets_ref[0, side : side + 1, :], counts_ref[0, :, side : side + 1], side
        )
        pick_ref[:, side * slots : (side + 1) * slots] = here.astype(BF)
        degree = degree + jnp.sum(here, axis=1, keepdims=True)
    degree_ref[...] = degree

    scaled = (grad_ref[0].astype(F32) / degree).T
    high = scaled.astype(BF)
    rest = scaled - high.astype(F32)
    mid = rest.astype(BF)
    low = (rest - mid.astype(F32)).astype(BF)
    spread = jnp.dot(low, links_low, preferred_element_type=F32)
    spread = spread + jnp.dot(mid, links_low, preferred_element_type=F32)
    spread = spread + jnp.dot(high, links_low, preferred_element_type=F32)
    graph_grad = (scaled + spread).astype(BF)

    key = jnp.dot(masked, wk_ref[...], preferred_element_type=F32).T.astype(BF)
    query = jnp.dot(masked, wq_ref[...], preferred_element_type=F32).T.astype(BF)
    value_t = value_wide.T.astype(BF)
    grad_t = grad_ref[0].astype(F32).T.astype(BF)
    for place, item in enumerate((key, value_t, query, grad_t, graph_grad)):
        for head in range(HEADS):
            heads_ref[head, BLK + place * HD : BLK + (place + 1) * HD, :] = item[
                head * HD : (head + 1) * HD
            ]


def columns_kernel(graph_ref, x_ref, columns_ref):
    columns_ref[...] = x_ref[:, 0:BLK, :]


def attention_kernel(
    mask_ref, x_ref, back_ref, grad_ref, list_ref, keys, duo, expo, gprob, peak, top, total, inner,
    out_acc, q_acc, k_acc, v_acc,
):
    count = jnp.int32(0)
    for i in range(NB):
        for j in range(NB):
            list_ref[count] = i * NB + j
            count = count + mask_ref[0, i, j]
    for u in range(UNROLL):
        list_ref[count + u] = NB * NB
    steps = lax.div(count + (UNROLL - 1), jnp.int32(UNROLL))
    duo[...] = jnp.zeros_like(duo)
    k_acc[...] = jnp.zeros_like(k_acc)
    v_acc[...] = jnp.zeros_like(v_acc)
    for b in range(NB):
        keys[b] = x_ref[b, BLK : BLK + 64, :].T
        duo[b, 0:HD, 0:BLK] = x_ref[b, BLK + 64 : BLK + 96, :]
        duo[b, HD : 2 * HD, BLK : 2 * BLK] = x_ref[b, BLK + 96 : BLK + 128, :]

    def pair(step, u):
        p = step * UNROLL + u
        index = list_ref[p]
        return p, lax.shift_right_logical(index, 4), lax.bitwise_and(index, 15)

    def scores(step, carry):
        before, m, l, d = carry
        parts = []
        for u in range(UNROLL):
            p, i, j = pair(step, u)
            both = jnp.dot(keys[j], duo[i], preferred_element_type=F32)
            s = both[:, :BLK]
            parts.append((p, i, s, both[:, BLK:], jnp.max(s, axis=0, keepdims=True)))
        for p, i, s, g, high in parts:
            same = i == before
            m_old = jnp.where(same, m, LOWEST)
            m = jnp.maximum(m_old, high)
            fade = jnp.exp2((m_old - m) * EXP_SCALE)
            e = jnp.exp2((s - m) * EXP_SCALE)
            l = jnp.where(same, l, 0.0) * fade + jnp.sum(e, axis=0, keepdims=True)
            d = jnp.where(same, d, 0.0) * fade + jnp.sum(e * g, axis=0, keepdims=True)
            expo[p] = e
            gprob[p] = g
            peak[p] = m
            top[i] = m
            total[i] = l
            inner[i] = d
            before = i
        return before, m, l, d

    zero = jnp.zeros((1, BLK), F32)
    lax.fori_loop(0, steps, scores, (jnp.int32(-1), zero, zero, zero))

    def grads(step, carry):
        before, o, q = carry
        for u in range(UNROLL):
            p, i, j = pair(step, u)
            share = 1.0 / total[i]
            prob = expo[p] * (jnp.exp2((peak[p] - top[i]) * EXP_SCALE) * share)
            low = prob.astype(BF)
            ds = (prob * (gprob[p] - inner[i] * share) * SCALE).astype(BF)
            same = i == before
            o = jnp.where(same, o, 0.0) + jnp.dot(
                x_ref[j, BLK + 32 : BLK + 64, :], low, preferred_element_type=F32
            )
            q = jnp.where(same, q, 0.0) + jnp.dot(
                x_ref[j, BLK : BLK + 32, :], ds, preferred_element_type=F32
            )
            out_acc[i] = o
            q_acc[i] = q
            k_acc[j] += lax.dot_general(
                duo[i, 0:HD, 0:BLK], ds, (((1,), (1,)), ((), ())), preferred_element_type=F32
            )
            v_acc[j] += lax.dot_general(
                duo[i, HD : 2 * HD, BLK : 2 * BLK], low, (((1,), (1,)), ((), ())),
                preferred_element_type=F32,
            )
            before = i
        return before, o, q

    wide = jnp.zeros((HD, BLK), F32)
    lax.fori_loop(0, steps, grads, (jnp.int32(-1), wide, wide))

    for b in range(NB):
        cols = slice(b * BLK, (b + 1) * BLK)
        back_ref[b] = out_acc[b].astype(BF)
        grad_ref[0:32, cols] = q_acc[b].astype(BF)
        grad_ref[32:64, cols] = k_acc[b].astype(BF)
        grad_ref[64:96, cols] = (
            v_acc[b].astype(BF).astype(F32) + x_ref[b, BLK + 128 : BLK + 160, :].astype(F32)
        ).astype(BF)


def weights_kernel(
    grad_ref, own_ref, down_ref, right_ref, far_ref, part_ref, full,
):
    group = group_of(lax.axis_index("seq"))
    pairs = (((own_ref, 0), (down_ref, 2)), ((right_ref, 1), (far_ref, 3)))
    for pair in pairs:
        columns = [ref[...].reshape(NB * ROWS, 128) for ref, _ in pair]
        both = jnp.dot(
            grad_ref[...], jnp.concatenate(columns, axis=1), preferred_element_type=F32
        )
        for n, (_, flip) in enumerate(pair):
            full[lax.bitwise_xor(group, flip)] = both[:, n * 128 : (n + 1) * 128]
    for lane in range(4):
        for half in range(2):
            part_ref[lane * 2 + half] = full[lane, half * CHUNK : (half + 1) * CHUNK, :]


def chip_kernel(both_ref, sum_ref):
    start = lax.bitwise_and(lax.axis_index("dp"), 1) * NEAR
    sum_ref[...] = both_ref[pl.ds(start, NEAR)] + both_ref[pl.ds(2 * NEAR + start, NEAR)]


def near_kernel(terms_ref, att_ref, sum_ref, att_out):
    att_out[...] = att_ref[...]
    sum_ref[...] = (terms_ref[0] + terms_ref[1]) + (terms_ref[2] + terms_ref[3])


def far_kernel(back_ref, terms_ref, copies_ref):
    total = (terms_ref[0] + terms_ref[1]) + (terms_ref[2] + terms_ref[3])
    for n in range(NEAR):
        copies_ref[n] = total


def output_kernel(all_ref, q_ref, k_ref, v_ref, full):
    for lane in range(4):
        for half in range(2):
            rows = slice(half * CHUNK, (half + 1) * CHUNK)
            full[rows, lane * 128 : (lane + 1) * 128] = all_ref[lane * 2 + half]
    for place, ref in enumerate((q_ref, k_ref, v_ref)):
        ref[...] = full[place * HD : (place + 1) * HD, :]


def graph_kernel(pick_ref, local_ref, degree_ref, lower_ref, upper_ref, graph_ref):
    rows = jnp.concatenate([lower_ref[0], upper_ref[0]], axis=0)
    border = jnp.dot(pick_ref[...], rows, preferred_element_type=F32)
    graph_ref[...] = (local_ref[...] + border) / degree_ref[...]


def mixed_kernel(att_ref, graph_ref, mixed_ref):
    attended = att_ref[...].reshape(WIDTH, ROWS).astype(F32).T
    mixed_ref[0] = (attended + graph_ref[...]).astype(BF)


def call(kernel, name, shapes, in_specs, scratch=(), limit=16, flops=0, moved=0):
    out = tuple(jax.ShapeDtypeStruct(shape, kind) for shape, kind in shapes)
    return pl.pallas_call(
        kernel,
        out_shape=out,
        in_specs=in_specs,
        out_specs=tuple(VM for _ in out),
        scratch_shapes=scratch,
        compiler_params=pltpu.CompilerParams(vmem_limit_bytes=limit * 1024 * 1024),
        cost_estimate=pl.CostEstimate(flops=flops, bytes_accessed=moved, transcendentals=0),
        name=name,
    )


def on_device(
    features, mask_token, w_query, w_key, w_value, block_mask, masked_ids, adjacency, boundary_ids,
    boundary_counts, boundary_targets, grad_out,
):
    clusters = lax.axis_size("dp")
    slots = boundary_ids.shape[2]
    sources = (
        masked_ids, boundary_counts.transpose(0, 2, 1), mask_token, features, w_value,
        adjacency, boundary_ids, boundary_targets, grad_out, w_key, w_query,
    )
    heads, send_lower, send_upper, local, degree, pick = call(
        rows_kernel,
        "rows",
        [
            ((HEADS, BLK + 5 * HD, ROWS), BF),
            ((1, slots, WIDTH), BF),
            ((1, slots, WIDTH), BF),
            ((ROWS, WIDTH), F32),
            ((ROWS, 1), F32),
            ((ROWS, 2 * slots), BF),
        ],
        [pl.BlockSpec(memory_space=pltpu.HBM)] * len(sources),
        scratch=[pltpu.VMEM(item.shape, item.dtype) for item in sources]
        + [pltpu.SemaphoreType.DMA((len(sources),))],
        flops=400_000_000,
        moved=3_000_000,
    )(*[pltpu.with_memory_space_constraint(item, pltpu.HBM) for item in sources])

    x = lax.all_to_all(heads, "seq", split_axis=0, concat_axis=0, tiled=True)
    up = [(c, c + 1) for c in range(clusters - 1)]
    lower = lax.ppermute(send_lower, "dp", up)
    upper = lax.ppermute(send_upper, "dp", [(b, a) for a, b in up])
    (graph,) = call(
        graph_kernel,
        "graph",
        [((ROWS, WIDTH), F32)],
        [VM] * 5,
        flops=20_000_000,
        moved=1_000_000,
    )(pick, local, degree, lower, upper)
    (columns,) = call(
        columns_kernel,
        "columns",
        [((NB, BLK, 128), BF)],
        [ANY, VM],
        flops=100_000,
        moved=1_000_000,
    )(graph, x)

    def neighbour(down, right, odd):
        def turn(n):
            return ((n + odd) ^ 1) - odd

        return lax.ppermute(
            columns,
            "seq",
            [
                (4 * y + x, 4 * ((turn(y) if down else y) % 4) + (turn(x) if right else x) % 4)
                for y in range(4)
                for x in range(4)
            ],
        )

    parts = [columns, neighbour(1, 0, 0), neighbour(0, 1, 0), neighbour(1, 1, 1)]

    back, grads = call(
        attention_kernel,
        "attention",
        [((NB, HD, BLK), BF), ((3 * HD, NB * BLK), BF)],
        [SM, VM],
        scratch=[
            pltpu.SMEM((SLOTS + UNROLL,), jnp.int32),
            pltpu.VMEM((NB, BLK, 2 * HD), BF),
            pltpu.VMEM((NB + 1, 2 * HD, 2 * BLK), BF),
            pltpu.VMEM((SLOTS, BLK, BLK), F32),
            pltpu.VMEM((SLOTS, BLK, BLK), F32),
            pltpu.VMEM((SLOTS, 1, BLK), F32),
            pltpu.VMEM((NB + 1, 1, BLK), F32),
            pltpu.VMEM((NB + 1, 1, BLK), F32),
            pltpu.VMEM((NB + 1, 1, BLK), F32),
            pltpu.VMEM((NB + 1, HD, BLK), F32),
            pltpu.VMEM((NB + 1, HD, BLK), F32),
            pltpu.VMEM((NB, HD, BLK), F32),
            pltpu.VMEM((NB, HD, BLK), F32),
        ],
        limit=44,
        flops=5_000_000_000,
        moved=20_000_000,
    )(block_mask, x)

    (part,) = call(
        weights_kernel,
        "weights",
        [((2 * NEAR, CHUNK, 128), F32)],
        [VM] * 5,
        scratch=[pltpu.VMEM((4, 3 * HD, 128), F32)],
        flops=200_000_000,
        moved=3_000_000,
    )(grads, *parts)
    cores = [[c, c + 1] for c in range(0, clusters, 2)]
    span = 2 * NEAR
    near = [
        [g * span + 2 * n + core for n in range(NEAR)]
        for g in range(clusters // span)
        for core in range(2)
    ]
    far = [[g * span + n for g in range(clusters // span)] for n in range(span)]

    def exchange(item, groups):
        return lax.all_to_all(
            item, "dp", split_axis=0, concat_axis=0, tiled=True, axis_index_groups=groups
        )

    def gather(item, groups):
        return lax.all_gather(item, "dp", axis=0, tiled=True, axis_index_groups=groups)

    (chip_sum,) = call(
        chip_kernel,
        "chip_sum",
        [((NEAR, CHUNK, 128), F32)],
        [VM],
        flops=100_000,
        moved=300_000,
    )(gather(part, cores))
    near_sum, back = call(
        near_kernel,
        "near_sum",
        [((CHUNK, 128), F32), ((NB, HD, BLK), BF)],
        [VM, VM],
        flops=100_000,
        moved=300_000,
    )(exchange(chip_sum, near), back)
    back = lax.all_to_all(back, "seq", split_axis=0, concat_axis=0, tiled=True)
    terms = lax.all_gather(near_sum, "dp", axis=0, tiled=False, axis_index_groups=far)
    (copies,) = call(
        far_kernel,
        "far_sum",
        [((NEAR, CHUNK, 128), F32)],
        [ANY, VM],
        flops=100_000,
        moved=300_000,
    )(back, terms)
    reduced = gather(exchange(copies, near), cores)
    (mixed,) = call(
        mixed_kernel,
        "mixed",
        [((1, ROWS, WIDTH), BF)],
        [VM, VM],
        flops=20_000_000,
        moved=1_000_000,
    )(back, graph)

    grad_query, grad_key, grad_value = call(
        output_kernel,
        "outputs",
        [((HD, WIDTH), F32)] * 3,
        [VM],
        scratch=[pltpu.VMEM((3 * HD, WIDTH), F32)],
        flops=1_000_000,
        moved=1_000_000,
    )(reduced)
    return mixed, grad_query.T, grad_key.T, grad_value.T


def solution(mesh):
    placed = (
        P("dp", "seq", None),
        P(),
        P(),
        P(),
        P(),
        P("dp", None, None),
        P("dp", None),
        P("dp", "seq", None),
        P("dp", None, "seq"),
        P("dp", None, "seq"),
        P("dp", None, "seq"),
        P("dp", "seq", None),
    )
    return jax.shard_map(
        on_device,
        mesh=mesh,
        in_specs=placed,
        out_specs=(P("dp", "seq", None), P(None, "seq"), P(None, "seq"), P(None, "seq")),
        check_vma=False,
    )
```

```python
import jax
import jax.numpy as jnp
from jax import lax
from jax.experimental import pallas as pl
from jax.experimental.pallas import tpu as pltpu
from jax.sharding import PartitionSpec as P

HEADS = 16
NB = 16
BLK = 128
HD = 32
ROWS = 128
WIDTH = 512
UNROLL = 16
SLOTS = NB * NB + UNROLL
SCALE = HD**-0.5
LOG2E = 1.4426950408889634
EXP_SCALE = SCALE * LOG2E
LOWEST = -3e38
BF = jnp.bfloat16
F32 = jnp.float32
NEAR = 4
CHUNK = 48

SM = pl.BlockSpec(memory_space=pltpu.SMEM)
VM = pl.BlockSpec(memory_space=pltpu.VMEM)
ANY = pl.BlockSpec(memory_space=pl.ANY)
HBM = pl.BlockSpec(memory_space=pltpu.HBM)


def group_of(place):
    return (place // 4 % 2) * 2 + place % 2


def attach(targets, counts, side):
    slots = targets.shape[1]
    rows = lax.broadcasted_iota(jnp.int32, (ROWS, slots), 0)
    slot = lax.broadcasted_iota(jnp.int32, (ROWS, slots), 1)
    place = lax.axis_index("dp")
    inside = (place > 0) if side == 0 else (place < lax.axis_size("dp") - 1)
    limit = jnp.where(inside, counts, 0)
    return jnp.where((targets == rows) & (slot < limit), 1.0, 0.0)


def rows_kernel(*refs):
    sources, refs = refs[:11], refs[11:]
    heads_ref, lower_ref, upper_ref, local_ref, degree_ref, pick_ref = refs[:6]
    holds, sems = refs[6:17], refs[17]
    copies = [
        pltpu.make_async_copy(source, hold, sems.at[n])
        for n, (source, hold) in enumerate(zip(sources, holds))
    ]
    for copy in copies:
        copy.start()
    (
        ids_ref, counts_ref, token_ref, tokens_ref, wv_ref, links_ref, sends_ref, targets_ref,
        grad_ref, wk_ref, wq_ref,
    ) = holds
    for copy in copies[:5]:
        copy.wait()
    own = lax.axis_index("seq") * ROWS + lax.broadcasted_iota(jnp.int32, (ROWS, 128), 0)
    hit = own < 0
    for part in range(ids_ref.shape[1] // 128):
        hit = hit | (own == ids_ref[:, part * 128 : (part + 1) * 128])
    marked = jnp.max(jnp.where(hit, 1.0, 0.0), axis=1, keepdims=True) > 0
    masked = jnp.where(marked, token_ref[...].reshape(1, WIDTH).astype(F32), tokens_ref[0].astype(F32)).astype(BF)
    for head in range(HEADS):
        group = group_of(head)
        heads_ref[head, 0:BLK, :] = masked[:, group * 128 : (group + 1) * 128]

    value_wide = jnp.dot(masked, wv_ref[...], preferred_element_type=F32)
    value = value_wide.astype(BF)
    for copy in copies[5:]:
        copy.wait()
    links_low = links_ref[0].astype(F32).astype(BF)
    local_ref[...] = value.astype(F32) + jnp.dot(links_low, value, preferred_element_type=F32)
    slots = sends_ref.shape[2]
    rows = lax.broadcasted_iota(jnp.int32, (ROWS, slots), 0)
    for side, ref in ((0, lower_ref), (1, upper_ref)):
        onehot = jnp.where(sends_ref[0, side : side + 1, :] == rows, 1.0, 0.0).astype(BF)
        ref[0] = lax.dot_general(
            onehot, value, (((0,), (0,)), ((), ())), preferred_element_type=F32
        ).astype(BF)

    degree = 1.0 + jnp.sum(links_ref[0].astype(F32), axis=1, keepdims=True)
    for side in range(2):
        here = attach(
            targets_ref[0, side : side + 1, :], counts_ref[0, :, side : side + 1], side
        )
        pick_ref[:, side * slots : (side + 1) * slots] = here.astype(BF)
        degree = degree + jnp.sum(here, axis=1, keepdims=True)
    degree_ref[...] = degree

    scaled = (grad_ref[0].astype(F32) / degree).T
    high = scaled.astype(BF)
    rest = scaled - high.astype(F32)
    mid = rest.astype(BF)
    low = (rest - mid.astype(F32)).astype(BF)
    spread = jnp.dot(low, links_low, preferred_element_type=F32)
    spread = spread + jnp.dot(mid, links_low, preferred_element_type=F32)
    spread = spread + jnp.dot(high, links_low, preferred_element_type=F32)
    graph_grad = (scaled + spread).astype(BF)

    key = jnp.dot(masked, wk_ref[...], preferred_element_type=F32).T.astype(BF)
    query = jnp.dot(masked, wq_ref[...], preferred_element_type=F32).T.astype(BF)
    value_t = value_wide.T.astype(BF)
    grad_t = grad_ref[0].astype(F32).T.astype(BF)
    for place, item in enumerate((key, value_t, query, grad_t, graph_grad)):
        for head in range(HEADS):
            heads_ref[head, BLK + place * HD : BLK + (place + 1) * HD, :] = item[
                head * HD : (head + 1) * HD
            ]


def columns_kernel(graph_ref, x_ref, columns_ref):
    columns_ref[...] = x_ref[:, 0:BLK, :]


def attention_kernel(
    mask_ref, x_ref, back_hbm, grad_ref, back_ref, sem, list_ref, keys, duo, expo, gprob, peak, top, total, inner,
    out_acc, q_acc, k_acc, v_acc,
):
    count = jnp.int32(0)
    for i in range(NB):
        for j in range(NB):
            list_ref[count] = i * NB + j
            count = count + mask_ref[0, i, j]
    for u in range(UNROLL):
        list_ref[count + u] = NB * NB
    steps = lax.div(count + (UNROLL - 1), jnp.int32(UNROLL))
    duo[...] = jnp.zeros_like(duo)
    k_acc[...] = jnp.zeros_like(k_acc)
    v_acc[...] = jnp.zeros_like(v_acc)
    for b in range(NB):
        keys[b] = x_ref[b, BLK : BLK + 64, :].T
        duo[b, 0:HD, 0:BLK] = x_ref[b, BLK + 64 : BLK + 96, :]
        duo[b, HD : 2 * HD, BLK : 2 * BLK] = x_ref[b, BLK + 96 : BLK + 128, :]

    def pair(step, u):
        p = step * UNROLL + u
        index = list_ref[p]
        return p, lax.shift_right_logical(index, 4), lax.bitwise_and(index, 15)

    def scores(step, carry):
        before, m, l, d = carry
        parts = []
        for u in range(UNROLL):
            p, i, j = pair(step, u)
            both = jnp.dot(keys[j], duo[i], preferred_element_type=F32)
            s = both[:, :BLK]
            parts.append((p, i, s, both[:, BLK:], jnp.max(s, axis=0, keepdims=True)))
        for p, i, s, g, high in parts:
            same = i == before
            m_old = jnp.where(same, m, LOWEST)
            m = jnp.maximum(m_old, high)
            fade = jnp.exp2((m_old - m) * EXP_SCALE)
            e = jnp.exp2((s - m) * EXP_SCALE)
            l = jnp.where(same, l, 0.0) * fade + jnp.sum(e, axis=0, keepdims=True)
            d = jnp.where(same, d, 0.0) * fade + jnp.sum(e * g, axis=0, keepdims=True)
            expo[p] = e
            gprob[p] = g
            peak[p] = m
            top[i] = m
            total[i] = l
            inner[i] = d
            before = i
        return before, m, l, d

    zero = jnp.zeros((1, BLK), F32)
    lax.fori_loop(0, steps, scores, (jnp.int32(-1), zero, zero, zero))

    def grads(step, carry):
        before, o, q = carry
        for u in range(UNROLL):
            p, i, j = pair(step, u)
            share = 1.0 / total[i]
            prob = expo[p] * (jnp.exp2((peak[p] - top[i]) * EXP_SCALE) * share)
            low = prob.astype(BF)
            ds = (prob * (gprob[p] - inner[i] * share) * SCALE).astype(BF)
            same = i == before
            o = jnp.where(same, o, 0.0) + jnp.dot(
                x_ref[j, BLK + 32 : BLK + 64, :], low, preferred_element_type=F32
            )
            q = jnp.where(same, q, 0.0) + jnp.dot(
                x_ref[j, BLK : BLK + 32, :], ds, preferred_element_type=F32
            )
            out_acc[i] = o
            q_acc[i] = q
            k_acc[j] += lax.dot_general(
                duo[i, 0:HD, 0:BLK], ds, (((1,), (1,)), ((), ())), preferred_element_type=F32
            )
            v_acc[j] += lax.dot_general(
                duo[i, HD : 2 * HD, BLK : 2 * BLK], low, (((1,), (1,)), ((), ())),
                preferred_element_type=F32,
            )
            before = i
        return before, o, q

    wide = jnp.zeros((HD, BLK), F32)
    lax.fori_loop(0, steps, grads, (jnp.int32(-1), wide, wide))

    for b in range(NB):
        back_ref[b] = out_acc[b].astype(BF)
    copy = pltpu.make_async_copy(back_ref, back_hbm, sem)
    copy.start()
    for b in range(NB):
        cols = slice(b * BLK, (b + 1) * BLK)
        grad_ref[0:32, cols] = q_acc[b].astype(BF)
        grad_ref[32:64, cols] = k_acc[b].astype(BF)
        grad_ref[64:96, cols] = (
            v_acc[b].astype(BF).astype(F32) + x_ref[b, BLK + 128 : BLK + 160, :].astype(F32)
        ).astype(BF)
    copy.wait()


def weights_kernel(
    grad_ref, own_ref, down_ref, right_ref, far_ref, part_ref, full,
):
    group = group_of(lax.axis_index("seq"))
    pairs = (((own_ref, 0), (down_ref, 2)), ((right_ref, 1), (far_ref, 3)))
    for pair in pairs:
        columns = [ref[...].reshape(NB * ROWS, 128) for ref, _ in pair]
        both = jnp.dot(
            grad_ref[...], jnp.concatenate(columns, axis=1), preferred_element_type=F32
        )
        for n, (_, flip) in enumerate(pair):
            full[lax.bitwise_xor(group, flip)] = both[:, n * 128 : (n + 1) * 128]
    for lane in range(4):
        for half in range(2):
            part_ref[lane * 2 + half] = full[lane, half * CHUNK : (half + 1) * CHUNK, :]


def chip_kernel(both_ref, sum_ref):
    start = lax.bitwise_and(lax.axis_index("dp"), 1) * NEAR
    sum_ref[...] = both_ref[pl.ds(start, NEAR)] + both_ref[pl.ds(2 * NEAR + start, NEAR)]


def near_kernel(terms_ref, att_ref, sum_ref, att_out):
    sum_ref[...] = (terms_ref[0] + terms_ref[1]) + (terms_ref[2] + terms_ref[3])


def far_kernel(back_ref, terms_ref, copies_ref):
    total = (terms_ref[0] + terms_ref[1]) + (terms_ref[2] + terms_ref[3])
    for n in range(2 * NEAR):
        copies_ref[n] = total


def output_kernel(all_ref, q_ref, k_ref, v_ref, full):
    for lane in range(4):
        for half in range(2):
            rows = slice(half * CHUNK, (half + 1) * CHUNK)
            chunk = lane * 2 + half
            full[rows, lane * 128 : (lane + 1) * 128] = all_ref[chunk % NEAR, chunk // NEAR]
    for place, ref in enumerate((q_ref, k_ref, v_ref)):
        ref[...] = full[place * HD : (place + 1) * HD, :]


def graph_kernel(pick_ref, local_ref, degree_ref, lower_ref, upper_ref, graph_ref):
    rows = jnp.concatenate([lower_ref[0], upper_ref[0]], axis=0)
    border = jnp.dot(pick_ref[...], rows, preferred_element_type=F32)
    graph_ref[...] = (local_ref[...] + border) / degree_ref[...]


def mixed_kernel(att_ref, graph_ref, mixed_ref):
    attended = att_ref[...].reshape(WIDTH, ROWS).astype(F32).T
    mixed_ref[0] = (attended + graph_ref[...]).astype(BF)


def call(
    kernel, name, shapes, in_specs, scratch=(), limit=16, flops=0, moved=0, outs=None, aliases=None
):
    outs = outs or [VM] * len(shapes)
    return pl.pallas_call(
        kernel,
        out_shape=tuple(
            (pltpu.HBM if spec is HBM else jax.ShapeDtypeStruct)(shape, kind)
            for (shape, kind), spec in zip(shapes, outs)
        ),
        in_specs=in_specs,
        out_specs=tuple(outs),
        scratch_shapes=scratch,
        input_output_aliases=aliases or {},
        compiler_params=pltpu.CompilerParams(vmem_limit_bytes=limit * 1024 * 1024),
        cost_estimate=pl.CostEstimate(flops=flops, bytes_accessed=moved, transcendentals=0),
        name=name,
    )


def on_device(
    features, mask_token, w_query, w_key, w_value, block_mask, masked_ids, adjacency, boundary_ids,
    boundary_counts, boundary_targets, grad_out,
):
    clusters = lax.axis_size("dp")
    slots = boundary_ids.shape[2]
    sources = (
        masked_ids, boundary_counts.transpose(0, 2, 1), mask_token, features, w_value,
        adjacency, boundary_ids, boundary_targets, grad_out, w_key, w_query,
    )
    heads, send_lower, send_upper, local, degree, pick = call(
        rows_kernel,
        "rows",
        [
            ((HEADS, BLK + 5 * HD, ROWS), BF),
            ((1, slots, WIDTH), BF),
            ((1, slots, WIDTH), BF),
            ((ROWS, WIDTH), F32),
            ((ROWS, 1), F32),
            ((ROWS, 2 * slots), BF),
        ],
        [pl.BlockSpec(memory_space=pltpu.HBM)] * len(sources),
        scratch=[pltpu.VMEM(item.shape, item.dtype) for item in sources]
        + [pltpu.SemaphoreType.DMA((len(sources),))],
        flops=400_000_000,
        moved=3_000_000,
    )(*[pltpu.with_memory_space_constraint(item, pltpu.HBM) for item in sources])

    x = lax.all_to_all(heads, "seq", split_axis=0, concat_axis=0, tiled=True)
    up = [(c, c + 1) for c in range(clusters - 1)]
    lower = lax.ppermute(send_lower, "dp", up)
    upper = lax.ppermute(send_upper, "dp", [(b, a) for a, b in up])
    (graph,) = call(
        graph_kernel,
        "graph",
        [((ROWS, WIDTH), F32)],
        [VM] * 5,
        flops=20_000_000,
        moved=1_000_000,
    )(pick, local, degree, lower, upper)
    (columns,) = call(
        columns_kernel,
        "columns",
        [((NB, BLK, 128), BF)],
        [ANY, VM],
        flops=100_000,
        moved=1_000_000,
    )(graph, x)

    def neighbour(down, right, odd):
        def turn(n):
            return ((n + odd) ^ 1) - odd

        return lax.ppermute(
            columns,
            "seq",
            [
                (4 * y + x, 4 * ((turn(y) if down else y) % 4) + (turn(x) if right else x) % 4)
                for y in range(4)
                for x in range(4)
            ],
        )

    parts = [columns, neighbour(1, 0, 0), neighbour(0, 1, 0), neighbour(1, 1, 1)]

    back, grads = call(
        attention_kernel,
        "attention",
        [((NB, HD, BLK), BF), ((3 * HD, NB * BLK), BF)],
        [SM, VM],
        outs=[HBM, VM],
        scratch=[
            pltpu.VMEM((NB, HD, BLK), BF),
            pltpu.SemaphoreType.DMA,
            pltpu.SMEM((SLOTS + UNROLL,), jnp.int32),
            pltpu.VMEM((NB, BLK, 2 * HD), BF),
            pltpu.VMEM((NB + 1, 2 * HD, 2 * BLK), BF),
            pltpu.VMEM((SLOTS, BLK, BLK), F32),
            pltpu.VMEM((SLOTS, BLK, BLK), F32),
            pltpu.VMEM((SLOTS, 1, BLK), F32),
            pltpu.VMEM((NB + 1, 1, BLK), F32),
            pltpu.VMEM((NB + 1, 1, BLK), F32),
            pltpu.VMEM((NB + 1, 1, BLK), F32),
            pltpu.VMEM((NB + 1, HD, BLK), F32),
            pltpu.VMEM((NB + 1, HD, BLK), F32),
            pltpu.VMEM((NB, HD, BLK), F32),
            pltpu.VMEM((NB, HD, BLK), F32),
        ],
        limit=44,
        flops=5_000_000_000,
        moved=20_000_000,
    )(block_mask, x)

    (part,) = call(
        weights_kernel,
        "weights",
        [((2 * NEAR, CHUNK, 128), F32)],
        [VM] * 5,
        scratch=[pltpu.VMEM((4, 3 * HD, 128), F32)],
        flops=200_000_000,
        moved=3_000_000,
    )(grads, *parts)
    cores = [[c, c + 1] for c in range(0, clusters, 2)]
    span = 2 * NEAR
    near = [
        [g * span + 2 * n + core for n in range(NEAR)]
        for g in range(clusters // span)
        for core in range(2)
    ]
    far = [[g * span + n for g in range(clusters // span)] for n in range(span)]

    def exchange(item, groups):
        return lax.all_to_all(
            item, "dp", split_axis=0, concat_axis=0, tiled=True, axis_index_groups=groups
        )

    def gather(item, groups):
        return lax.all_gather(item, "dp", axis=0, tiled=True, axis_index_groups=groups)

    (chip_sum,) = call(
        chip_kernel,
        "chip_sum",
        [((NEAR, CHUNK, 128), F32)],
        [VM],
        flops=100_000,
        moved=300_000,
    )(gather(part, cores))
    near_sum, back = call(
        near_kernel,
        "near_sum",
        [((CHUNK, 128), F32), ((NB, HD, BLK), BF)],
        [VM, HBM],
        outs=[VM, HBM],
        aliases={1: 1},
        flops=100_000,
        moved=300_000,
    )(exchange(chip_sum, near), back)
    back = lax.all_to_all(back, "seq", split_axis=0, concat_axis=0, tiled=True)
    terms = lax.all_gather(near_sum, "dp", axis=0, tiled=False, axis_index_groups=far)
    (copies,) = call(
        far_kernel,
        "far_sum",
        [((2 * NEAR, CHUNK, 128), F32)],
        [ANY, VM],
        flops=100_000,
        moved=300_000,
    )(back, terms)
    block = [[g * span + n for n in range(span)] for g in range(clusters // span)]
    order = exchange(copies, block)
    reduced = order.reshape(NEAR, 2, CHUNK, 128)
    (mixed,) = call(
        mixed_kernel,
        "mixed",
        [((1, ROWS, WIDTH), BF)],
        [VM, VM],
        flops=20_000_000,
        moved=1_000_000,
    )(back, graph)

    grad_query, grad_key, grad_value = call(
        output_kernel,
        "outputs",
        [((HD, WIDTH), F32)] * 3,
        [VM],
        scratch=[pltpu.VMEM((3 * HD, WIDTH), F32)],
        flops=1_000_000,
        moved=1_000_000,
    )(reduced)
    return mixed, grad_query.T, grad_key.T, grad_value.T


def solution(mesh):
    placed = (
        P("dp", "seq", None),
        P(),
        P(),
        P(),
        P(),
        P("dp", None, None),
        P("dp", None),
        P("dp", "seq", None),
        P("dp", None, "seq"),
        P("dp", None, "seq"),
        P("dp", None, "seq"),
        P("dp", "seq", None),
    )
    return jax.shard_map(
        on_device,
        mesh=mesh,
        in_specs=placed,
        out_specs=(P("dp", "seq", None), P(None, "seq"), P(None, "seq"), P(None, "seq")),
        check_vma=False,
    )
```

```python
import jax
import jax.numpy as jnp
from jax import lax
from jax.experimental import pallas as pl
from jax.experimental.pallas import tpu as pltpu
from jax.sharding import PartitionSpec as P

HEADS = 16
NB = 16
BLK = 128
HD = 32
ROWS = 128
WIDTH = 512
UNROLL = 16
SLOTS = NB * NB + UNROLL
SCALE = HD**-0.5
LOG2E = 1.4426950408889634
EXP_SCALE = SCALE * LOG2E
LOWEST = -3e38
BF = jnp.bfloat16
F32 = jnp.float32
NEAR = 4
CHUNK = 48

SM = pl.BlockSpec(memory_space=pltpu.SMEM)
VM = pl.BlockSpec(memory_space=pltpu.VMEM)
ANY = pl.BlockSpec(memory_space=pl.ANY)
HBM = pl.BlockSpec(memory_space=pltpu.HBM)


def group_of(place):
    return (place // 4 % 2) * 2 + place % 2


def attach(targets, counts, side):
    slots = targets.shape[1]
    rows = lax.broadcasted_iota(jnp.int32, (ROWS, slots), 0)
    slot = lax.broadcasted_iota(jnp.int32, (ROWS, slots), 1)
    place = lax.axis_index("dp")
    inside = (place > 0) if side == 0 else (place < lax.axis_size("dp") - 1)
    limit = jnp.where(inside, counts, 0)
    return jnp.where((targets == rows) & (slot < limit), 1.0, 0.0)


def rows_kernel(*refs):
    sources, refs = refs[:11], refs[11:]
    heads_hbm, lower_ref, upper_ref, local_ref, degree_ref, pick_ref = refs[:6]
    holds, (sems, heads_ref, heads_sems) = refs[6:17], refs[17:]

    def leave(first, count, n):
        rows = pl.ds(first, count)
        copy = pltpu.make_async_copy(heads_ref.at[:, rows], heads_hbm.at[:, rows], heads_sems.at[n])
        copy.start()
        return copy

    def put(item, place):
        for head in range(HEADS):
            heads_ref[head, BLK + place * HD : BLK + (place + 1) * HD, :] = item[
                head * HD : (head + 1) * HD
            ]
        return leave(BLK + place * HD, HD, place)

    copies = [
        pltpu.make_async_copy(source, hold, sems.at[n])
        for n, (source, hold) in enumerate(zip(sources, holds))
    ]
    for copy in copies:
        copy.start()
    (
        ids_ref, counts_ref, token_ref, tokens_ref, wv_ref, links_ref, sends_ref, targets_ref,
        grad_ref, wk_ref, wq_ref,
    ) = holds
    for copy in copies[:5]:
        copy.wait()
    own = lax.axis_index("seq") * ROWS + lax.broadcasted_iota(jnp.int32, (ROWS, 128), 0)
    hit = own < 0
    for part in range(ids_ref.shape[1] // 128):
        hit = hit | (own == ids_ref[:, part * 128 : (part + 1) * 128])
    marked = jnp.max(jnp.where(hit, 1.0, 0.0), axis=1, keepdims=True) > 0
    masked = jnp.where(marked, token_ref[...].reshape(1, WIDTH).astype(F32), tokens_ref[0].astype(F32)).astype(BF)
    for head in range(HEADS):
        group = group_of(head)
        heads_ref[head, 0:BLK, :] = masked[:, group * 128 : (group + 1) * 128]

    leaving = [leave(0, BLK, 5)]
    value_wide = jnp.dot(masked, wv_ref[...], preferred_element_type=F32)
    value = value_wide.astype(BF)
    for copy in copies[5:]:
        copy.wait()
    key = jnp.dot(masked, wk_ref[...], preferred_element_type=F32).T.astype(BF)
    query = jnp.dot(masked, wq_ref[...], preferred_element_type=F32).T.astype(BF)
    leaving.append(put(value_wide.T.astype(BF), 1))
    leaving.append(put(grad_ref[0].astype(F32).T.astype(BF), 3))
    leaving.append(put(key, 0))
    leaving.append(put(query, 2))

    slots = sends_ref.shape[2]
    degree = 1.0 + jnp.sum(links_ref[0].astype(F32), axis=1, keepdims=True)
    for side in range(2):
        here = attach(
            targets_ref[0, side : side + 1, :], counts_ref[0, :, side : side + 1], side
        )
        pick_ref[:, side * slots : (side + 1) * slots] = here.astype(BF)
        degree = degree + jnp.sum(here, axis=1, keepdims=True)
    degree_ref[...] = degree

    links_low = links_ref[0].astype(F32).astype(BF)
    scaled = (grad_ref[0].astype(F32) / degree).T
    high = scaled.astype(BF)
    rest = scaled - high.astype(F32)
    mid = rest.astype(BF)
    low = (rest - mid.astype(F32)).astype(BF)
    spread = jnp.dot(low, links_low, preferred_element_type=F32)
    spread = spread + jnp.dot(mid, links_low, preferred_element_type=F32)
    spread = spread + jnp.dot(high, links_low, preferred_element_type=F32)
    leaving.append(put((scaled + spread).astype(BF), 4))

    local_ref[...] = value.astype(F32) + jnp.dot(links_low, value, preferred_element_type=F32)
    rows = lax.broadcasted_iota(jnp.int32, (ROWS, slots), 0)
    for side, ref in ((0, lower_ref), (1, upper_ref)):
        onehot = jnp.where(sends_ref[0, side : side + 1, :] == rows, 1.0, 0.0).astype(BF)
        ref[0] = lax.dot_general(
            onehot, value, (((0,), (0,)), ((), ())), preferred_element_type=F32
        ).astype(BF)
    for copy in leaving:
        copy.wait()


def columns_kernel(graph_ref, x_ref, columns_ref):
    columns_ref[...] = x_ref[:, 0:BLK, :]


def attention_kernel(
    mask_ref, x_ref, back_hbm, grad_ref, back_ref, sem, list_ref, keys, duo, expo, gprob, peak, top, total, inner,
    out_acc, q_acc, k_acc, v_acc,
):
    count = jnp.int32(0)
    for i in range(NB):
        for j in range(NB):
            list_ref[count] = i * NB + j
            count = count + mask_ref[0, i, j]
    for u in range(UNROLL):
        list_ref[count + u] = NB * NB
    steps = lax.div(count + (UNROLL - 1), jnp.int32(UNROLL))
    duo[...] = jnp.zeros_like(duo)
    k_acc[...] = jnp.zeros_like(k_acc)
    v_acc[...] = jnp.zeros_like(v_acc)
    for b in range(NB):
        keys[b] = x_ref[b, BLK : BLK + 64, :].T
        duo[b, 0:HD, 0:BLK] = x_ref[b, BLK + 64 : BLK + 96, :]
        duo[b, HD : 2 * HD, BLK : 2 * BLK] = x_ref[b, BLK + 96 : BLK + 128, :]

    def pair(step, u):
        p = step * UNROLL + u
        index = list_ref[p]
        return p, lax.shift_right_logical(index, 4), lax.bitwise_and(index, 15)

    def scores(step, carry):
        before, m, l, d = carry
        parts = []
        for u in range(UNROLL):
            p, i, j = pair(step, u)
            both = jnp.dot(keys[j], duo[i], preferred_element_type=F32)
            s = both[:, :BLK]
            parts.append((p, i, s, both[:, BLK:], jnp.max(s, axis=0, keepdims=True)))
        for p, i, s, g, high in parts:
            same = i == before
            m_old = jnp.where(same, m, LOWEST)
            m = jnp.maximum(m_old, high)
            fade = jnp.exp2((m_old - m) * EXP_SCALE)
            e = jnp.exp2((s - m) * EXP_SCALE)
            l = jnp.where(same, l, 0.0) * fade + jnp.sum(e, axis=0, keepdims=True)
            d = jnp.where(same, d, 0.0) * fade + jnp.sum(e * g, axis=0, keepdims=True)
            expo[p] = e
            gprob[p] = g
            peak[p] = m
            top[i] = m
            total[i] = l
            inner[i] = d
            before = i
        return before, m, l, d

    zero = jnp.zeros((1, BLK), F32)
    lax.fori_loop(0, steps, scores, (jnp.int32(-1), zero, zero, zero))

    def grads(step, carry):
        before, o, q = carry
        for u in range(UNROLL):
            p, i, j = pair(step, u)
            share = 1.0 / total[i]
            prob = expo[p] * (jnp.exp2((peak[p] - top[i]) * EXP_SCALE) * share)
            low = prob.astype(BF)
            ds = (prob * (gprob[p] - inner[i] * share) * SCALE).astype(BF)
            same = i == before
            o = jnp.where(same, o, 0.0) + jnp.dot(
                x_ref[j, BLK + 32 : BLK + 64, :], low, preferred_element_type=F32
            )
            q = jnp.where(same, q, 0.0) + jnp.dot(
                x_ref[j, BLK : BLK + 32, :], ds, preferred_element_type=F32
            )
            out_acc[i] = o
            q_acc[i] = q
            k_acc[j] += lax.dot_general(
                duo[i, 0:HD, 0:BLK], ds, (((1,), (1,)), ((), ())), preferred_element_type=F32
            )
            v_acc[j] += lax.dot_general(
                duo[i, HD : 2 * HD, BLK : 2 * BLK], low, (((1,), (1,)), ((), ())),
                preferred_element_type=F32,
            )
            before = i
        return before, o, q

    wide = jnp.zeros((HD, BLK), F32)
    lax.fori_loop(0, steps, grads, (jnp.int32(-1), wide, wide))

    for b in range(NB):
        back_ref[b] = out_acc[b].astype(BF)
    copy = pltpu.make_async_copy(back_ref, back_hbm, sem)
    copy.start()
    for b in range(NB):
        cols = slice(b * BLK, (b + 1) * BLK)
        grad_ref[0:32, cols] = q_acc[b].astype(BF)
        grad_ref[32:64, cols] = k_acc[b].astype(BF)
        grad_ref[64:96, cols] = (
            v_acc[b].astype(BF).astype(F32) + x_ref[b, BLK + 128 : BLK + 160, :].astype(F32)
        ).astype(BF)
    copy.wait()


def weights_kernel(
    grad_ref, own_ref, down_ref, right_ref, far_ref, part_ref, full,
):
    group = group_of(lax.axis_index("seq"))
    pairs = (((own_ref, 0), (down_ref, 2)), ((right_ref, 1), (far_ref, 3)))
    for pair in pairs:
        columns = [ref[...].reshape(NB * ROWS, 128) for ref, _ in pair]
        both = jnp.dot(
            grad_ref[...], jnp.concatenate(columns, axis=1), preferred_element_type=F32
        )
        for n, (_, flip) in enumerate(pair):
            full[lax.bitwise_xor(group, flip)] = both[:, n * 128 : (n + 1) * 128]
    for lane in range(4):
        for half in range(2):
            part_ref[lane * 2 + half] = full[lane, half * CHUNK : (half + 1) * CHUNK, :]


def chip_kernel(both_ref, sum_ref):
    start = lax.bitwise_and(lax.axis_index("dp"), 1) * NEAR
    sum_ref[...] = both_ref[pl.ds(start, NEAR)] + both_ref[pl.ds(2 * NEAR + start, NEAR)]


def near_kernel(terms_ref, att_ref, sum_ref, att_out):
    sum_ref[...] = (terms_ref[0] + terms_ref[1]) + (terms_ref[2] + terms_ref[3])


def far_kernel(terms_ref, att_ref, graph_ref, copies_ref, mixed_ref):
    total = (terms_ref[0] + terms_ref[1]) + (terms_ref[2] + terms_ref[3])
    for n in range(2 * NEAR):
        copies_ref[n] = total
    attended = att_ref[...].reshape(WIDTH, ROWS).astype(F32).T
    mixed_ref[0] = (attended + graph_ref[...]).astype(BF)


def output_kernel(all_ref, q_ref, k_ref, v_ref, full):
    for lane in range(4):
        for half in range(2):
            rows = slice(half * CHUNK, (half + 1) * CHUNK)
            chunk = lane * 2 + half
            full[rows, lane * 128 : (lane + 1) * 128] = all_ref[chunk % NEAR, chunk // NEAR]
    for place, ref in enumerate((q_ref, k_ref, v_ref)):
        ref[...] = full[place * HD : (place + 1) * HD, :]


def graph_kernel(pick_ref, local_ref, degree_ref, lower_ref, upper_ref, graph_ref):
    rows = jnp.concatenate([lower_ref[0], upper_ref[0]], axis=0)
    border = jnp.dot(pick_ref[...], rows, preferred_element_type=F32)
    graph_ref[...] = (local_ref[...] + border) / degree_ref[...]


def call(
    kernel, name, shapes, in_specs, scratch=(), limit=16, flops=0, moved=0, outs=None, aliases=None
):
    outs = outs or [VM] * len(shapes)
    return pl.pallas_call(
        kernel,
        out_shape=tuple(
            (pltpu.HBM if spec is HBM else jax.ShapeDtypeStruct)(shape, kind)
            for (shape, kind), spec in zip(shapes, outs)
        ),
        in_specs=in_specs,
        out_specs=tuple(outs),
        scratch_shapes=scratch,
        input_output_aliases=aliases or {},
        compiler_params=pltpu.CompilerParams(vmem_limit_bytes=limit * 1024 * 1024),
        cost_estimate=pl.CostEstimate(flops=flops, bytes_accessed=moved, transcendentals=0),
        name=name,
    )


def on_device(
    features, mask_token, w_query, w_key, w_value, block_mask, masked_ids, adjacency, boundary_ids,
    boundary_counts, boundary_targets, grad_out,
):
    clusters = lax.axis_size("dp")
    slots = boundary_ids.shape[2]
    sources = (
        masked_ids, boundary_counts.transpose(0, 2, 1), mask_token, features, w_value,
        adjacency, boundary_ids, boundary_targets, grad_out, w_key, w_query,
    )
    heads, send_lower, send_upper, local, degree, pick = call(
        rows_kernel,
        "rows",
        [
            ((HEADS, BLK + 5 * HD, ROWS), BF),
            ((1, slots, WIDTH), BF),
            ((1, slots, WIDTH), BF),
            ((ROWS, WIDTH), F32),
            ((ROWS, 1), F32),
            ((ROWS, 2 * slots), BF),
        ],
        [pl.BlockSpec(memory_space=pltpu.HBM)] * len(sources),
        scratch=[pltpu.VMEM(item.shape, item.dtype) for item in sources]
        + [
            pltpu.SemaphoreType.DMA((len(sources),)),
            pltpu.VMEM((HEADS, BLK + 5 * HD, ROWS), BF),
            pltpu.SemaphoreType.DMA((6,)),
        ],
        outs=[HBM] + [VM] * 5,
        flops=400_000_000,
        moved=3_000_000,
    )(*[pltpu.with_memory_space_constraint(item, pltpu.HBM) for item in sources])

    x = lax.all_to_all(heads, "seq", split_axis=0, concat_axis=0, tiled=True)
    up = [(c, c + 1) for c in range(clusters - 1)]
    lower = lax.ppermute(send_lower, "dp", up)
    upper = lax.ppermute(send_upper, "dp", [(b, a) for a, b in up])
    (graph,) = call(
        graph_kernel,
        "graph",
        [((ROWS, WIDTH), F32)],
        [VM] * 5,
        flops=20_000_000,
        moved=1_000_000,
    )(pick, local, degree, lower, upper)
    (columns,) = call(
        columns_kernel,
        "columns",
        [((NB, BLK, 128), BF)],
        [ANY, VM],
        flops=100_000,
        moved=1_000_000,
    )(graph, x)

    def neighbour(down, right, odd):
        def turn(n):
            return ((n + odd) ^ 1) - odd

        return lax.ppermute(
            columns,
            "seq",
            [
                (4 * y + x, 4 * ((turn(y) if down else y) % 4) + (turn(x) if right else x) % 4)
                for y in range(4)
                for x in range(4)
            ],
        )

    parts = [columns, neighbour(1, 0, 0), neighbour(0, 1, 0), neighbour(1, 1, 1)]

    back, grads = call(
        attention_kernel,
        "attention",
        [((NB, HD, BLK), BF), ((3 * HD, NB * BLK), BF)],
        [SM, VM],
        outs=[HBM, VM],
        scratch=[
            pltpu.VMEM((NB, HD, BLK), BF),
            pltpu.SemaphoreType.DMA,
            pltpu.SMEM((SLOTS + UNROLL,), jnp.int32),
            pltpu.VMEM((NB, BLK, 2 * HD), BF),
            pltpu.VMEM((NB + 1, 2 * HD, 2 * BLK), BF),
            pltpu.VMEM((SLOTS, BLK, BLK), F32),
            pltpu.VMEM((SLOTS, BLK, BLK), F32),
            pltpu.VMEM((SLOTS, 1, BLK), F32),
            pltpu.VMEM((NB + 1, 1, BLK), F32),
            pltpu.VMEM((NB + 1, 1, BLK), F32),
            pltpu.VMEM((NB + 1, 1, BLK), F32),
            pltpu.VMEM((NB + 1, HD, BLK), F32),
            pltpu.VMEM((NB + 1, HD, BLK), F32),
            pltpu.VMEM((NB, HD, BLK), F32),
            pltpu.VMEM((NB, HD, BLK), F32),
        ],
        limit=44,
        flops=5_000_000_000,
        moved=20_000_000,
    )(block_mask, x)

    (part,) = call(
        weights_kernel,
        "weights",
        [((2 * NEAR, CHUNK, 128), F32)],
        [VM] * 5,
        scratch=[pltpu.VMEM((4, 3 * HD, 128), F32)],
        flops=200_000_000,
        moved=3_000_000,
    )(grads, *parts)
    cores = [[c, c + 1] for c in range(0, clusters, 2)]
    span = 2 * NEAR
    near = [
        [g * span + 2 * n + core for n in range(NEAR)]
        for g in range(clusters // span)
        for core in range(2)
    ]
    far = [[g * span + n for g in range(clusters // span)] for n in range(span)]

    def exchange(item, groups):
        return lax.all_to_all(
            item, "dp", split_axis=0, concat_axis=0, tiled=True, axis_index_groups=groups
        )

    def gather(item, groups):
        return lax.all_gather(item, "dp", axis=0, tiled=True, axis_index_groups=groups)

    (chip_sum,) = call(
        chip_kernel,
        "chip_sum",
        [((NEAR, CHUNK, 128), F32)],
        [VM],
        flops=100_000,
        moved=300_000,
    )(gather(part, cores))
    near_sum, back = call(
        near_kernel,
        "near_sum",
        [((CHUNK, 128), F32), ((NB, HD, BLK), BF)],
        [VM, HBM],
        outs=[VM, HBM],
        aliases={1: 1},
        flops=100_000,
        moved=300_000,
    )(exchange(chip_sum, near), back)
    back = lax.all_to_all(back, "seq", split_axis=0, concat_axis=0, tiled=True)
    terms = lax.all_gather(near_sum, "dp", axis=0, tiled=False, axis_index_groups=far)
    copies, mixed = call(
        far_kernel,
        "far_sum",
        [((2 * NEAR, CHUNK, 128), F32), ((1, ROWS, WIDTH), BF)],
        [VM, VM, VM],
        flops=100_000,
        moved=300_000,
    )(terms, back, graph)
    block = [[g * span + n for n in range(span)] for g in range(clusters // span)]
    order = exchange(copies, block)
    reduced = order.reshape(NEAR, 2, CHUNK, 128)
    grad_query, grad_key, grad_value = call(
        output_kernel,
        "outputs",
        [((HD, WIDTH), F32)] * 3,
        [VM],
        scratch=[pltpu.VMEM((3 * HD, WIDTH), F32)],
        flops=1_000_000,
        moved=1_000_000,
    )(reduced)
    return mixed, grad_query.T, grad_key.T, grad_value.T


def solution(mesh):
    placed = (
        P("dp", "seq", None),
        P(),
        P(),
        P(),
        P(),
        P("dp", None, None),
        P("dp", None),
        P("dp", "seq", None),
        P("dp", None, "seq"),
        P("dp", None, "seq"),
        P("dp", None, "seq"),
        P("dp", "seq", None),
    )
    return jax.shard_map(
        on_device,
        mesh=mesh,
        in_specs=placed,
        out_specs=(P("dp", "seq", None), P(None, "seq"), P(None, "seq"), P(None, "seq")),
        check_vma=False,
    )
```

```python
import jax
import jax.numpy as jnp
from jax import lax
from jax.experimental import pallas as pl
from jax.experimental.pallas import tpu as pltpu
from jax.sharding import PartitionSpec as P

HEADS = 16
NB = 16
BLK = 128
HD = 32
ROWS = 128
WIDTH = 512
UNROLL = 16
SLOTS = NB * NB + UNROLL
SCALE = HD**-0.5
LOG2E = 1.4426950408889634
EXP_SCALE = SCALE * LOG2E
LOWEST = -3e38
BF = jnp.bfloat16
F32 = jnp.float32
NEAR = 4
CHUNK = 48

SM = pl.BlockSpec(memory_space=pltpu.SMEM)
VM = pl.BlockSpec(memory_space=pltpu.VMEM)
ANY = pl.BlockSpec(memory_space=pl.ANY)
HBM = pl.BlockSpec(memory_space=pltpu.HBM)


def group_of(place):
    return (place // 4 % 2) * 2 + place % 2


def attach(targets, counts, side):
    slots = targets.shape[1]
    rows = lax.broadcasted_iota(jnp.int32, (ROWS, slots), 0)
    slot = lax.broadcasted_iota(jnp.int32, (ROWS, slots), 1)
    place = lax.axis_index("dp")
    inside = (place > 0) if side == 0 else (place < lax.axis_size("dp") - 1)
    limit = jnp.where(inside, counts, 0)
    return jnp.where((targets == rows) & (slot < limit), 1.0, 0.0)


def rows_kernel(*refs):
    sources, refs = refs[:11], refs[11:]
    heads_hbm, lower_ref, upper_ref, local_ref, degree_ref, pick_ref = refs[:6]
    holds, (sems, heads_ref, heads_sems) = refs[6:17], refs[17:]

    def leave(first, count, n):
        rows = pl.ds(first, count)
        copy = pltpu.make_async_copy(heads_ref.at[:, rows], heads_hbm.at[:, rows], heads_sems.at[n])
        copy.start()
        return copy

    def put(item, place):
        for head in range(HEADS):
            heads_ref[head, BLK + place * HD : BLK + (place + 1) * HD, :] = item[
                head * HD : (head + 1) * HD
            ]
        return leave(BLK + place * HD, HD, place)

    copies = [
        pltpu.make_async_copy(source, hold, sems.at[n])
        for n, (source, hold) in enumerate(zip(sources, holds))
    ]
    for copy in copies:
        copy.start()
    (
        ids_ref, counts_ref, token_ref, tokens_ref, wv_ref, links_ref, sends_ref, targets_ref,
        grad_ref, wk_ref, wq_ref,
    ) = holds
    for copy in copies[:5]:
        copy.wait()
    own = lax.axis_index("seq") * ROWS + lax.broadcasted_iota(jnp.int32, (ROWS, 128), 0)
    hit = own < 0
    for part in range(ids_ref.shape[1] // 128):
        hit = hit | (own == ids_ref[:, part * 128 : (part + 1) * 128])
    marked = jnp.max(jnp.where(hit, 1.0, 0.0), axis=1, keepdims=True) > 0
    masked = jnp.where(marked, token_ref[...].reshape(1, WIDTH).astype(F32), tokens_ref[0].astype(F32)).astype(BF)
    for head in range(HEADS):
        group = group_of(head)
        heads_ref[head, 0:BLK, :] = masked[:, group * 128 : (group + 1) * 128]

    leaving = [leave(0, BLK, 5)]
    value_wide = jnp.dot(masked, wv_ref[...], preferred_element_type=F32)
    value = value_wide.astype(BF)
    for copy in copies[5:]:
        copy.wait()
    key = jnp.dot(masked, wk_ref[...], preferred_element_type=F32).T.astype(BF)
    query = jnp.dot(masked, wq_ref[...], preferred_element_type=F32).T.astype(BF)
    leaving.append(put(value_wide.T.astype(BF), 1))
    leaving.append(put(grad_ref[0].astype(F32).T.astype(BF), 3))
    leaving.append(put(key, 0))
    leaving.append(put(query, 2))

    slots = sends_ref.shape[2]
    degree = 1.0 + jnp.sum(links_ref[0].astype(F32), axis=1, keepdims=True)
    for side in range(2):
        here = attach(
            targets_ref[0, side : side + 1, :], counts_ref[0, :, side : side + 1], side
        )
        pick_ref[:, side * slots : (side + 1) * slots] = here.astype(BF)
        degree = degree + jnp.sum(here, axis=1, keepdims=True)
    degree_ref[...] = degree

    links_low = links_ref[0].astype(F32).astype(BF)
    scaled = (grad_ref[0].astype(F32) / degree).T
    high = scaled.astype(BF)
    rest = scaled - high.astype(F32)
    mid = rest.astype(BF)
    low = (rest - mid.astype(F32)).astype(BF)
    spread = jnp.dot(low, links_low, preferred_element_type=F32)
    spread = spread + jnp.dot(mid, links_low, preferred_element_type=F32)
    spread = spread + jnp.dot(high, links_low, preferred_element_type=F32)
    leaving.append(put((scaled + spread).astype(BF), 4))

    local_ref[...] = value.astype(F32) + jnp.dot(links_low, value, preferred_element_type=F32)
    rows = lax.broadcasted_iota(jnp.int32, (ROWS, slots), 0)
    for side, ref in ((0, lower_ref), (1, upper_ref)):
        onehot = jnp.where(sends_ref[0, side : side + 1, :] == rows, 1.0, 0.0).astype(BF)
        ref[0] = lax.dot_general(
            onehot, value, (((0,), (0,)), ((), ())), preferred_element_type=F32
        ).astype(BF)
    for copy in leaving:
        copy.wait()


def columns_kernel(graph_ref, x_ref, columns_ref):
    columns_ref[...] = x_ref[:, 0:BLK, :]


def attention_kernel(
    mask_ref, x_ref, back_hbm, grad_ref, back_ref, sem, list_ref, keys, duo, expo, gprob, peak, top, total, inner,
    out_acc, q_acc, k_acc, v_acc,
):
    count = jnp.int32(0)
    for i in range(NB):
        for j in range(NB):
            list_ref[count] = i * NB + j
            count = count + mask_ref[0, i, j]
    for u in range(UNROLL):
        list_ref[count + u] = NB * NB
    steps = lax.div(count + (UNROLL - 1), jnp.int32(UNROLL))
    duo[...] = jnp.zeros_like(duo)
    k_acc[...] = jnp.zeros_like(k_acc)
    v_acc[...] = jnp.zeros_like(v_acc)
    for b in range(NB):
        keys[b] = x_ref[b, BLK : BLK + 64, :].T
        duo[b, 0:HD, 0:BLK] = x_ref[b, BLK + 64 : BLK + 96, :]
        duo[b, HD : 2 * HD, BLK : 2 * BLK] = x_ref[b, BLK + 96 : BLK + 128, :]

    def pair(step, u):
        p = step * UNROLL + u
        index = list_ref[p]
        return p, lax.shift_right_logical(index, 4), lax.bitwise_and(index, 15)

    def scores(step, carry):
        before, m, l, d = carry
        parts = []
        for u in range(UNROLL):
            p, i, j = pair(step, u)
            both = jnp.dot(keys[j], duo[i], preferred_element_type=F32)
            s = both[:, :BLK]
            parts.append((p, i, s, both[:, BLK:], jnp.max(s, axis=0, keepdims=True)))
        for p, i, s, g, high in parts:
            same = i == before
            m_old = jnp.where(same, m, LOWEST)
            m = jnp.maximum(m_old, high)
            fade = jnp.exp2((m_old - m) * EXP_SCALE)
            e = jnp.exp2((s - m) * EXP_SCALE)
            l = jnp.where(same, l, 0.0) * fade + jnp.sum(e, axis=0, keepdims=True)
            d = jnp.where(same, d, 0.0) * fade + jnp.sum(e * g, axis=0, keepdims=True)
            expo[p] = e
            gprob[p] = g
            peak[p] = m
            top[i] = m
            total[i] = l
            inner[i] = d
            before = i
        return before, m, l, d

    zero = jnp.zeros((1, BLK), F32)
    lax.fori_loop(0, steps, scores, (jnp.int32(-1), zero, zero, zero))

    def grads(step, carry):
        before, o, q = carry
        for u in range(UNROLL):
            p, i, j = pair(step, u)
            share = 1.0 / total[i]
            prob = expo[p] * (jnp.exp2((peak[p] - top[i]) * EXP_SCALE) * share)
            low = prob.astype(BF)
            ds = (prob * (gprob[p] - inner[i] * share) * SCALE).astype(BF)
            same = i == before
            o = jnp.where(same, o, 0.0) + jnp.dot(
                x_ref[j, BLK + 32 : BLK + 64, :], low, preferred_element_type=F32
            )
            q = jnp.where(same, q, 0.0) + jnp.dot(
                x_ref[j, BLK : BLK + 32, :], ds, preferred_element_type=F32
            )
            out_acc[i] = o
            q_acc[i] = q
            k_acc[j] += lax.dot_general(
                duo[i, 0:HD, 0:BLK], ds, (((1,), (1,)), ((), ())), preferred_element_type=F32
            )
            v_acc[j] += lax.dot_general(
                duo[i, HD : 2 * HD, BLK : 2 * BLK], low, (((1,), (1,)), ((), ())),
                preferred_element_type=F32,
            )
            before = i
        return before, o, q

    wide = jnp.zeros((HD, BLK), F32)
    lax.fori_loop(0, steps, grads, (jnp.int32(-1), wide, wide))

    for b in range(NB):
        back_ref[b] = out_acc[b].astype(BF)
    copy = pltpu.make_async_copy(back_ref, back_hbm, sem)
    copy.start()
    for b in range(NB):
        cols = slice(b * BLK, (b + 1) * BLK)
        grad_ref[0:32, cols] = q_acc[b].astype(BF)
        grad_ref[32:64, cols] = k_acc[b].astype(BF)
        grad_ref[64:96, cols] = (
            v_acc[b].astype(BF).astype(F32) + x_ref[b, BLK + 128 : BLK + 160, :].astype(F32)
        ).astype(BF)
    copy.wait()


def weights_kernel(
    grad_ref, own_ref, down_ref, right_ref, far_ref, part_ref, full,
):
    group = group_of(lax.axis_index("seq"))
    pairs = (((own_ref, 0), (down_ref, 2)), ((right_ref, 1), (far_ref, 3)))
    for pair in pairs:
        columns = [ref[...].reshape(NB * ROWS, 128) for ref, _ in pair]
        both = jnp.dot(
            grad_ref[...], jnp.concatenate(columns, axis=1), preferred_element_type=F32
        )
        for n, (_, flip) in enumerate(pair):
            full[lax.bitwise_xor(group, flip)] = both[:, n * 128 : (n + 1) * 128]
    for lane in range(4):
        for half in range(2):
            chunk = lane * 2 + half
            part_ref[chunk % NEAR * 2 + chunk // NEAR] = full[
                lane, half * CHUNK : (half + 1) * CHUNK, :
            ]


def near_kernel(terms_ref, att_ref, sum_ref, att_out):
    pairs = [terms_ref[2 * n] + terms_ref[2 * n + 1] for n in range(NEAR)]
    sum_ref[...] = (pairs[0] + pairs[1]) + (pairs[2] + pairs[3])


def far_kernel(terms_ref, att_ref, graph_ref, copies_ref, mixed_ref):
    total = (terms_ref[0] + terms_ref[1]) + (terms_ref[2] + terms_ref[3])
    for n in range(2 * NEAR):
        copies_ref[n] = total
    attended = att_ref[...].reshape(WIDTH, ROWS).astype(F32).T
    mixed_ref[0] = (attended + graph_ref[...]).astype(BF)


def output_kernel(all_ref, q_ref, k_ref, v_ref, full):
    for lane in range(4):
        for half in range(2):
            rows = slice(half * CHUNK, (half + 1) * CHUNK)
            chunk = lane * 2 + half
            full[rows, lane * 128 : (lane + 1) * 128] = all_ref[chunk % NEAR, chunk // NEAR]
    for place, ref in enumerate((q_ref, k_ref, v_ref)):
        ref[...] = full[place * HD : (place + 1) * HD, :]


def graph_kernel(pick_ref, local_ref, degree_ref, lower_ref, upper_ref, graph_ref):
    rows = jnp.concatenate([lower_ref[0], upper_ref[0]], axis=0)
    border = jnp.dot(pick_ref[...], rows, preferred_element_type=F32)
    graph_ref[...] = (local_ref[...] + border) / degree_ref[...]


def call(
    kernel, name, shapes, in_specs, scratch=(), limit=16, flops=0, moved=0, outs=None, aliases=None
):
    outs = outs or [VM] * len(shapes)
    return pl.pallas_call(
        kernel,
        out_shape=tuple(
            (pltpu.HBM if spec is HBM else jax.ShapeDtypeStruct)(shape, kind)
            for (shape, kind), spec in zip(shapes, outs)
        ),
        in_specs=in_specs,
        out_specs=tuple(outs),
        scratch_shapes=scratch,
        input_output_aliases=aliases or {},
        compiler_params=pltpu.CompilerParams(vmem_limit_bytes=limit * 1024 * 1024),
        cost_estimate=pl.CostEstimate(flops=flops, bytes_accessed=moved, transcendentals=0),
        name=name,
    )


def on_device(
    features, mask_token, w_query, w_key, w_value, block_mask, masked_ids, adjacency, boundary_ids,
    boundary_counts, boundary_targets, grad_out,
):
    clusters = lax.axis_size("dp")
    slots = boundary_ids.shape[2]
    sources = (
        masked_ids, boundary_counts.transpose(0, 2, 1), mask_token, features, w_value,
        adjacency, boundary_ids, boundary_targets, grad_out, w_key, w_query,
    )
    heads, send_lower, send_upper, local, degree, pick = call(
        rows_kernel,
        "rows",
        [
            ((HEADS, BLK + 5 * HD, ROWS), BF),
            ((1, slots, WIDTH), BF),
            ((1, slots, WIDTH), BF),
            ((ROWS, WIDTH), F32),
            ((ROWS, 1), F32),
            ((ROWS, 2 * slots), BF),
        ],
        [pl.BlockSpec(memory_space=pltpu.HBM)] * len(sources),
        scratch=[pltpu.VMEM(item.shape, item.dtype) for item in sources]
        + [
            pltpu.SemaphoreType.DMA((len(sources),)),
            pltpu.VMEM((HEADS, BLK + 5 * HD, ROWS), BF),
            pltpu.SemaphoreType.DMA((6,)),
        ],
        outs=[HBM] + [VM] * 5,
        flops=400_000_000,
        moved=3_000_000,
    )(*[pltpu.with_memory_space_constraint(item, pltpu.HBM) for item in sources])

    x = lax.all_to_all(heads, "seq", split_axis=0, concat_axis=0, tiled=True)
    up = [(c, c + 1) for c in range(clusters - 1)]
    lower = lax.ppermute(send_lower, "dp", up)
    upper = lax.ppermute(send_upper, "dp", [(b, a) for a, b in up])
    (graph,) = call(
        graph_kernel,
        "graph",
        [((ROWS, WIDTH), F32)],
        [VM] * 5,
        flops=20_000_000,
        moved=1_000_000,
    )(pick, local, degree, lower, upper)
    (columns,) = call(
        columns_kernel,
        "columns",
        [((NB, BLK, 128), BF)],
        [ANY, VM],
        flops=100_000,
        moved=1_000_000,
    )(graph, x)

    def neighbour(down, right, odd):
        def turn(n):
            return ((n + odd) ^ 1) - odd

        return lax.ppermute(
            columns,
            "seq",
            [
                (4 * y + x, 4 * ((turn(y) if down else y) % 4) + (turn(x) if right else x) % 4)
                for y in range(4)
                for x in range(4)
            ],
        )

    parts = [columns, neighbour(1, 0, 0), neighbour(0, 1, 0), neighbour(1, 1, 1)]

    back, grads = call(
        attention_kernel,
        "attention",
        [((NB, HD, BLK), BF), ((3 * HD, NB * BLK), BF)],
        [SM, VM],
        outs=[HBM, VM],
        scratch=[
            pltpu.VMEM((NB, HD, BLK), BF),
            pltpu.SemaphoreType.DMA,
            pltpu.SMEM((SLOTS + UNROLL,), jnp.int32),
            pltpu.VMEM((NB, BLK, 2 * HD), BF),
            pltpu.VMEM((NB + 1, 2 * HD, 2 * BLK), BF),
            pltpu.VMEM((SLOTS, BLK, BLK), F32),
            pltpu.VMEM((SLOTS, BLK, BLK), F32),
            pltpu.VMEM((SLOTS, 1, BLK), F32),
            pltpu.VMEM((NB + 1, 1, BLK), F32),
            pltpu.VMEM((NB + 1, 1, BLK), F32),
            pltpu.VMEM((NB + 1, 1, BLK), F32),
            pltpu.VMEM((NB + 1, HD, BLK), F32),
            pltpu.VMEM((NB + 1, HD, BLK), F32),
            pltpu.VMEM((NB, HD, BLK), F32),
            pltpu.VMEM((NB, HD, BLK), F32),
        ],
        limit=44,
        flops=5_000_000_000,
        moved=20_000_000,
    )(block_mask, x)

    (part,) = call(
        weights_kernel,
        "weights",
        [((2 * NEAR, CHUNK, 128), F32)],
        [VM] * 5,
        scratch=[pltpu.VMEM((4, 3 * HD, 128), F32)],
        flops=200_000_000,
        moved=3_000_000,
    )(grads, *parts)
    cores = [[c, c + 1] for c in range(0, clusters, 2)]
    span = 2 * NEAR
    near = [
        [g * span + 2 * n + core for n in range(NEAR)]
        for g in range(clusters // span)
        for core in range(2)
    ]
    far = [[g * span + n for g in range(clusters // span)] for n in range(span)]

    def exchange(item, groups):
        return lax.all_to_all(
            item, "dp", split_axis=0, concat_axis=0, tiled=True, axis_index_groups=groups
        )

    def gather(item, groups):
        return lax.all_gather(item, "dp", axis=0, tiled=True, axis_index_groups=groups)

    block = [[g * span + n for n in range(span)] for g in range(clusters // span)]
    near_sum, back = call(
        near_kernel,
        "near_sum",
        [((CHUNK, 128), F32), ((NB, HD, BLK), BF)],
        [VM, HBM],
        outs=[VM, HBM],
        aliases={1: 1},
        flops=100_000,
        moved=300_000,
    )(exchange(part, block), back)
    back = lax.all_to_all(back, "seq", split_axis=0, concat_axis=0, tiled=True)
    terms = lax.all_gather(near_sum, "dp", axis=0, tiled=False, axis_index_groups=far)
    copies, mixed = call(
        far_kernel,
        "far_sum",
        [((2 * NEAR, CHUNK, 128), F32), ((1, ROWS, WIDTH), BF)],
        [VM, VM, VM],
        flops=100_000,
        moved=300_000,
    )(terms, back, graph)
    order = exchange(copies, block)
    reduced = order.reshape(NEAR, 2, CHUNK, 128)
    grad_query, grad_key, grad_value = call(
        output_kernel,
        "outputs",
        [((HD, WIDTH), F32)] * 3,
        [VM],
        scratch=[pltpu.VMEM((3 * HD, WIDTH), F32)],
        flops=1_000_000,
        moved=1_000_000,
    )(reduced)
    return mixed, grad_query.T, grad_key.T, grad_value.T


def solution(mesh):
    placed = (
        P("dp", "seq", None),
        P(),
        P(),
        P(),
        P(),
        P("dp", None, None),
        P("dp", None),
        P("dp", "seq", None),
        P("dp", None, "seq"),
        P("dp", None, "seq"),
        P("dp", None, "seq"),
        P("dp", "seq", None),
    )
    return jax.shard_map(
        on_device,
        mesh=mesh,
        in_specs=placed,
        out_specs=(P("dp", "seq", None), P(None, "seq"), P(None, "seq"), P(None, "seq")),
        check_vma=False,
    )
```
